32 devices in a mesh: parts: 2 (over y), dp: 2 (over x), tensor: 4 (over z), sub: 2 (over core).
Axes of the slice: x: 2, y: 2, z: 4, core: 2. Of those that a mesh axis runs over, the one named last changes fastest.
Arguments:
- acts: bfloat16 [512, 5120], P(('parts', 'tensor'), ('dp', 'sub')), parts along dimension 0, may hold values from -6 to 6
- frozen_weight: bfloat16 [5120, 25600], P(('dp', 'sub'), 'tensor'), may hold values from -0.078125 to 0.078125
- adapter_down_maps: bfloat16 [8, 5120, 64], P(('parts', 'tensor'), ('dp', 'sub')), parts along dimension 0, may hold values from -0.078125 to 0.078125
- adapter_up_maps: bfloat16 [8, 64, 25600], P(('parts', 'dp', 'sub'), None, 'tensor'), parts along dimension 0, may hold values from -0.75 to 0.75
- down_first_moment: float32 [8, 5120, 64], P(('parts', 'tensor'), ('dp', 'sub')), parts along dimension 0, may hold values from -0.75 to 0.75
- down_second_moment: float32 [8, 5120, 64], P(('parts', 'tensor'), ('dp', 'sub')), parts along dimension 0, may hold values from 0.0001 to 0.01
- up_first_moment: float32 [8, 64, 25600], P(('parts', 'dp', 'sub'), None, 'tensor'), parts along dimension 0, may hold values from -0.078125 to 0.078125
- up_second_moment: float32 [8, 64, 25600], P(('parts', 'dp', 'sub'), None, 'tensor'), parts along dimension 0, may hold values from 1e-06 to 0.0001
- readout: bfloat16 [512, 25600], P(('parts', 'dp', 'sub'), 'tensor'), parts along dimension 0, may hold values from -0.0390625 to 0.0390625
- adapter_index_rows: int32 [512, 1], P('parts'), parts along dimension 0, may hold values from 0 to 3; in each aligned block of 64 rows (0 to 63, 64 to 127, ...) at most 32 rows name the same one
- preference_pair_rows: int32 [256, 2], P(('parts', 'dp', 'sub')), parts along dimension 0, may hold values from 0 to 63, as said below
Outputs:
- updated_down_maps: bfloat16 [8, 5120, 64], P(('parts', 'tensor'), ('dp', 'sub')), parts along dimension 0
- updated_down_first: float32 [8, 5120, 64], P(('parts', 'tensor'), ('dp', 'sub')), parts along dimension 0
- updated_down_second: float32 [8, 5120, 64], P(('parts', 'tensor'), ('dp', 'sub')), parts along dimension 0
- updated_up_maps: bfloat16 [8, 64, 25600], P(('parts', 'dp', 'sub'), None, 'tensor'), parts along dimension 0
- updated_up_first: float32 [8, 64, 25600], P(('parts', 'dp', 'sub'), None, 'tensor'), parts along dimension 0
- updated_up_second: float32 [8, 64, 25600], P(('parts', 'dp', 'sub'), None, 'tensor'), parts along dimension 0
The draws below stay inside these ranges and needn't reach their ends.
There are 2 independent parts, one for each index of `parts`. The reference program is written for one: setup_inputs(seed, part) draws one part's arguments, and reference() takes and returns one part's arrays. A program takes and returns all parts, laid end to end along the dimension named above; an argument that names none is the same for every part. Nothing has to cross between parts.
Inputs may be any that keep to these rules, and one draw needn't show every extreme that they name: `adapter_index_rows`: within the rows of one group (aligned blocks of 64 rows) no adapter is named by more than 32 rows, and in every draw some group has an adapter named by exactly 32 rows. `preference_pair_rows`: the pairs of group q are rows q * (32) to (q + 1) * 32 - 1; together their two columns name every row index of the group exactly once.
All inputs are finite; a program needn't handle non-finite values.
Results may differ from the reference program's by a relative error of at most 0.0034.
Values may be sent and summed in bfloat16 or wider, within the bound.
A program may use at most 128 MiB of HBM per device.

```python
import math
import jax
import jax.numpy as jnp
import numpy as np
from jax import lax

MODEL_WIDTH = 5120
HIDDEN_UNITS = 25600
ADAPTER_RANK = 64
GROUP_ROWS = 64
GROUPS = 4
ADAPTER_COUNT = 4
ROWS = 256
CAPACITY = 32


def draw_preference_pair_rows(key, part):
    key = jax.random.fold_in(key, 11)
    group_keys = jax.random.split(key, ROWS // GROUP_ROWS)
    orders = jax.vmap(lambda group_key: jax.random.permutation(group_key, GROUP_ROWS))(group_keys)
    return orders.reshape(ROWS // 2, 2).astype(jnp.int32)


def block_scale(stream_key, extent, shards, smallest, high):
    level, own = 1.0, jax.random.fold_in(stream_key, 6)
    for position, parts in shards:
        heights = jnp.exp(jax.random.uniform(jax.random.fold_in(own, position), (parts,), jnp.float32, smallest / len(shards), high / len(shards)))
        level = level * jnp.repeat(heights, extent[position] // parts).reshape([-1 if axis == position else 1 for axis in range(len(extent))])
    return level


def shared_out(own_key, own, number, rows, number_of, top, most, slope):
    ranking = jax.random.permutation(own_key, number_of)
    heavy_load, ordinary = load_shares(number_of, rows * top, most, slope, True), load_shares(number_of, rows * top, most, slope, False)
    places = jnp.arange(number_of)

    def named(tallies, offset_by):
        used = int((tallies > 0).sum())
        fixed = max(1, used // 4)
        shifted = fixed + (places - fixed + offset_by * (used - fixed)) % max(1, number_of - fixed)
        return jnp.zeros((number_of,), jnp.int32).at[ranking[jnp.where(places < fixed, places, shifted)]].set(jnp.asarray(tallies, jnp.int32))

    tallies = jnp.where(number % 4 == 0, named(heavy_load, number // 4), named(ordinary, number - number // 4 - 1))
    mixed = jax.random.permutation(jax.random.fold_in(own, 3), number_of)
    source_of, taker = mixed[0:number_of // 2 * 2:2], mixed[1:number_of // 2 * 2:2]
    slack = jnp.minimum(tallies[source_of] - 1, most - tallies[taker]) // 2
    slack = jnp.where((source_of == ranking[0]) | (taker == ranking[0]) | (tallies[taker] == 0), 0, jnp.maximum(slack, 0))
    shifted = jax.random.randint(jax.random.fold_in(own, 4), (number_of // 2,), 0, 1 << 20) % (slack + 1)
    tallies = tallies.at[source_of].add(-shifted).at[taker].add(shifted)
    labels = jnp.searchsorted(jnp.cumsum(tallies), jnp.arange(rows * top), side="right").astype(jnp.int32)
    table = labels.reshape(top, rows).T
    table = table[jax.random.permutation(jax.random.fold_in(own, 1), rows)]
    offset_by = jax.random.randint(jax.random.fold_in(own, 2), (rows, 1), 0, top)
    return jnp.take_along_axis(table, (jnp.arange(top)[None, :] + offset_by) % top, axis=1)


def load_shares(number_of, total, bound, slope, full):
    loads = [(1 << 20) // math.isqrt(standing ** slope) + 1 for standing in range(1, number_of + 1)]
    largest = bound if full else min(bound, max(-(-total // number_of), total * loads[0] // sum(loads)))
    least = 1 if total - largest >= number_of - 1 else 0
    given, rest = [largest] + [least] * (number_of - 1), total - largest - least * (number_of - 1)
    while rest > 0:
        candidates = [i for i in range(1, number_of) if given[i] < largest] or [i for i in range(1, number_of) if given[i] < bound]
        whole, left = sum([loads[i] for i in candidates]), rest
        for i in candidates:
            more = min(bound - given[i], max(1, left * loads[i] // whole), rest)
            given[i] = given[i] + more
            rest = rest - more
    return np.array(given)


def bell_draw(stream_key, shape, scale, bound, shards=(), kind=jnp.bfloat16):
    gain = block_scale(stream_key, shape, shards, -0.22, 0.18) if shards else 1.0
    drawn = jax.random.normal(stream_key, shape, jnp.float32) * scale * gain
    return jnp.minimum(jnp.maximum(drawn, -bound), bound).astype(kind)


def setup_inputs(seed: int = 0, part: int = 0) -> dict:
    key_list = jax.random.split(jax.random.key(seed), 12)
    part_keys = jax.random.split(jax.random.fold_in(key_list[11], part), 12)
    acts = bell_draw(part_keys[0], (ROWS, MODEL_WIDTH), 1.0, 6.0, ((0, 4), (1, 4)))
    frozen_weight = bell_draw(key_list[1], (MODEL_WIDTH, HIDDEN_UNITS), MODEL_WIDTH ** -0.5, 0.078125, ((0, 4), (1, 4)))
    adapter_down_maps = bell_draw(part_keys[2], (ADAPTER_COUNT, MODEL_WIDTH, ADAPTER_RANK), MODEL_WIDTH ** -0.5, 0.078125, ((0, 4), (1, 4)))
    adapter_up_maps = bell_draw(part_keys[3], (ADAPTER_COUNT, ADAPTER_RANK, HIDDEN_UNITS), ADAPTER_RANK ** -0.5, 0.75, ((0, 4), (2, 4)))
    down_first_moment = bell_draw(part_keys[4], (ADAPTER_COUNT, MODEL_WIDTH, ADAPTER_RANK), 0.05, 0.75, ((0, 4), (1, 4)), jnp.float32)
    down_second_moment = jnp.clip(jnp.exp(math.log(0.01) - 4.6051702 * jax.random.uniform(part_keys[5], (ADAPTER_COUNT, MODEL_WIDTH, ADAPTER_RANK), jnp.float32) ** block_scale(part_keys[5], (ADAPTER_COUNT, MODEL_WIDTH, ADAPTER_RANK), ((0, 4), (1, 4)), -0.2, 0.2)), 0.0001, 0.01)
    up_first_moment = bell_draw(part_keys[6], (ADAPTER_COUNT, ADAPTER_RANK, HIDDEN_UNITS), 0.005, 0.078125, ((0, 4), (2, 4)), jnp.float32)
    up_second_moment = jnp.clip(jnp.exp(math.log(0.0001) - 4.6051702 * jax.random.uniform(part_keys[7], (ADAPTER_COUNT, ADAPTER_RANK, HIDDEN_UNITS), jnp.float32) ** block_scale(part_keys[7], (ADAPTER_COUNT, ADAPTER_RANK, HIDDEN_UNITS), ((0, 4), (2, 4)), -0.2, 0.2)), 9.999999974752427e-07, 0.0001)
    readout = bell_draw(part_keys[8], (ROWS, HIDDEN_UNITS), HIDDEN_UNITS ** -0.5, 0.0390625, ((0, 4), (1, 4)))
    adapter_index_rows_keys = jax.random.split(jax.random.fold_in(part_keys[9], 1), ROWS // GROUP_ROWS)
    adapter_index_rows_turns = jax.random.permutation(jax.random.fold_in(part_keys[9], 3), ROWS // GROUP_ROWS)
    adapter_index_rows = jax.vmap(lambda own, number: shared_out(jax.random.fold_in(part_keys[9], 2), own, number, GROUP_ROWS, ADAPTER_COUNT, 1, CAPACITY, 2))(adapter_index_rows_keys, adapter_index_rows_turns).reshape((ROWS, 1))
    preference_pair_rows = draw_preference_pair_rows(jax.random.fold_in(jax.random.fold_in(key_list[11], part), 71), part)
    return dict(acts=acts, frozen_weight=frozen_weight, adapter_down_maps=adapter_down_maps, adapter_up_maps=adapter_up_maps, down_first_moment=down_first_moment, down_second_moment=down_second_moment, up_first_moment=up_first_moment, up_second_moment=up_second_moment, readout=readout, adapter_index_rows=adapter_index_rows, preference_pair_rows=preference_pair_rows)


adapter_scale = 2.0
beta_pref = 0.1
learn_rate = 0.001
first_decay = 0.9
second_decay = 0.95
first_fix = 1.0 - 2.656139888758747e-05
second_fix = 1.0 - 0.005920529220334
adam_eps = 1e-08

def swish_slope(pre_act):
    sigmoid_of = jax.nn.sigmoid(pre_act)
    return sigmoid_of * (1.0 + pre_act * (1.0 - sigmoid_of))

def moment_update_step(param, mean_old, square_old, grad):
    new_mean = first_decay * mean_old + (1.0 - first_decay) * grad
    new_square = second_decay * square_old + (1.0 - second_decay) * grad * grad
    update_step = new_mean / first_fix / (jnp.sqrt(new_square / second_fix) + adam_eps)
    new_param = (param.astype(jnp.float32) - learn_rate * update_step).astype(jnp.bfloat16)
    return (new_param, new_mean, new_square)

def reference(acts, frozen_weight, adapter_down_maps, adapter_up_maps, down_first_moment, down_second_moment, up_first_moment, up_second_moment, readout, adapter_index_rows, preference_pair_rows):
    block_column_width = MODEL_WIDTH // GROUPS
    adapter_of = adapter_index_rows[:, 0]
    catalog = jnp.arange(ADAPTER_COUNT, dtype=jnp.int32)
    membership = (adapter_of[:, None] == catalog[None, :]).astype(jnp.float32)

    def block_terms(running, block_index):
        base_run, shrink_run = running
        block_offset = (block_index * block_column_width).astype(jnp.int32)
        block_rows = lax.dynamic_slice_in_dim(acts, block_offset, block_column_width, 1)
        block_base = lax.dynamic_slice_in_dim(frozen_weight, block_offset, block_column_width, 0)
        down_block_part = lax.dynamic_slice_in_dim(adapter_down_maps, block_offset, block_column_width, 1)
        base_term = jnp.dot(block_rows, block_base, preferred_element_type=jnp.float32).astype(jnp.bfloat16)
        products = jnp.einsum('rd,adk->rak', block_rows.astype(jnp.float32), down_block_part.astype(jnp.float32))
        shrink_term = lax.optimization_barrier(jnp.sum(products * membership[:, :, None], axis=1)).astype(jnp.bfloat16)
        base_term, shrink_term = lax.optimization_barrier((base_term, shrink_term))
        return ((base_run + base_term.astype(jnp.float32), shrink_run + shrink_term.astype(jnp.float32)), None)
    start_pair = (jnp.zeros((ROWS, HIDDEN_UNITS), jnp.float32), jnp.zeros((ROWS, ADAPTER_RANK), jnp.float32))
    (frozen_sum, shrink), _ = lax.scan(block_terms, start_pair, jnp.arange(GROUPS, dtype=jnp.int32))
    shrink_low = shrink.astype(jnp.bfloat16)
    scatter_rows = (membership[:, :, None] * shrink_low.astype(jnp.float32)[:, None, :]).reshape(ROWS, ADAPTER_COUNT * ADAPTER_RANK).astype(jnp.bfloat16)
    up_flattened = adapter_up_maps.reshape(ADAPTER_COUNT * ADAPTER_RANK, HIDDEN_UNITS)
    widen_rows = jnp.dot(scatter_rows, up_flattened, preferred_element_type=jnp.float32).astype(jnp.bfloat16)
    policy_scores = frozen_sum + adapter_scale * widen_rows.astype(jnp.float32)
    read_float = readout.astype(jnp.float32)
    score_policy = lax.optimization_barrier(jnp.sum(read_float * jax.nn.silu(policy_scores), axis=1))
    score_base = lax.optimization_barrier(jnp.sum(read_float * jax.nn.silu(frozen_sum), axis=1))
    margin_rows = score_policy - score_base
    pair_group = jnp.arange(ROWS // 2, dtype=jnp.int32) // (GROUP_ROWS // 2)
    chosen = pair_group * GROUP_ROWS + preference_pair_rows[:, 0]
    rejected = pair_group * GROUP_ROWS + preference_pair_rows[:, 1]
    margin = beta_pref * (margin_rows[chosen] - margin_rows[rejected])
    weight = beta_pref * jax.nn.sigmoid(-margin)
    row_grad = jnp.zeros((ROWS,), jnp.float32).at[chosen].add(-weight).at[rejected].add(weight)
    output_gradient = (row_grad[:, None] * read_float * swish_slope(policy_scores)).astype(jnp.bfloat16)
    up_gradient = adapter_scale * jnp.dot(scatter_rows.T, output_gradient, preferred_element_type=jnp.float32).reshape(ADAPTER_COUNT, ADAPTER_RANK, HIDDEN_UNITS)
    every_returned = jnp.dot(output_gradient, up_flattened.T, preferred_element_type=jnp.float32).reshape(ROWS, ADAPTER_COUNT, ADAPTER_RANK)
    rank_gradient = (adapter_scale * lax.optimization_barrier(jnp.sum(every_returned * membership[:, :, None], axis=1))).astype(jnp.bfloat16)
    spread_back = (membership[:, :, None] * rank_gradient.astype(jnp.float32)[:, None, :]).reshape(ROWS, ADAPTER_COUNT * ADAPTER_RANK).astype(jnp.bfloat16)
    down_gradient = jnp.dot(acts.T, spread_back, preferred_element_type=jnp.float32).reshape(MODEL_WIDTH, ADAPTER_COUNT, ADAPTER_RANK).transpose(1, 0, 2)
    updated_down_maps, updated_down_first, updated_down_second = moment_update_step(adapter_down_maps, down_first_moment, down_second_moment, down_gradient)
    updated_up_maps, updated_up_first, updated_up_second = moment_update_step(adapter_up_maps, up_first_moment, up_second_moment, up_gradient)
    return (updated_down_maps, updated_down_first, updated_down_second, updated_up_maps, updated_up_first, updated_up_second)
```

```python
import functools

import jax
import jax.numpy as jnp
from jax import lax
from jax.experimental import pallas as pl
from jax.experimental.pallas import tpu as pltpu
from jax.sharding import PartitionSpec as P

adapter_scale = 2.0
beta_pref = 0.1
learn_rate = 0.001
first_decay = 0.9
second_decay = 0.95
first_fix = 1.0 - 2.656139888758747e-05
second_fix = 1.0 - 0.005920529220334
adam_eps = 1e-08


def swish_slope(pre_act):
    sigmoid_of = jax.nn.sigmoid(pre_act)
    return sigmoid_of * (1.0 + pre_act * (1.0 - sigmoid_of))


def moment_update_step(param, mean_old, square_old, grad):
    new_mean = first_decay * mean_old + (1.0 - first_decay) * grad
    new_square = second_decay * square_old + (1.0 - second_decay) * grad * grad
    update_step = new_mean / first_fix / (jnp.sqrt(new_square / second_fix) + adam_eps)
    new_param = (param.astype(jnp.float32) - learn_rate * update_step).astype(jnp.bfloat16)
    return (new_param, new_mean, new_square)


def body(
    acts,
    frozen_weight,
    adapter_down_maps,
    adapter_up_maps,
    down_first_moment,
    down_second_moment,
    up_first_moment,
    up_second_moment,
    readout,
    adapter_index_rows,
    preference_pair_rows,
):
    group_count = lax.axis_size(("dp", "sub"))
    group_index = lax.axis_index(("dp", "sub"))
    tensor_index = lax.axis_index("tensor")
    reduced_rank_output = adapter_down_maps.shape[2]
    local_down_maps = adapter_down_maps.shape[0]
    local_up_maps = adapter_up_maps.shape[0]
    adapters = local_up_maps * group_count
    group_rows = readout.shape[0]
    columns = readout.shape[1]
    ids_all = adapter_index_rows[:, 0]
    catalog = jnp.arange(adapters, dtype=jnp.int32)
    member_all = (ids_all[:, None] == catalog[None, :]).astype(jnp.float32)
    member_mine = lax.dynamic_slice_in_dim(
        member_all, tensor_index * local_down_maps, local_down_maps, 1
    )
    rows_all = lax.all_gather(acts, "tensor", axis=0, tiled=True)
    base_part = jnp.dot(rows_all, frozen_weight, preferred_element_type=jnp.float32)
    down_maps_total = lax.all_gather(adapter_down_maps, "tensor", axis=0, tiled=True)
    products = jnp.einsum(
        "rd,adk->rak", rows_all, down_maps_total, preferred_element_type=jnp.float32
    )
    shrink_part = jnp.sum(products * member_all[:, :, None], axis=1)
    base_terms = base_part.astype(jnp.bfloat16).reshape(group_count, group_rows, columns)
    shrink_terms = shrink_part.astype(jnp.bfloat16).reshape(
        group_count, group_rows, reduced_rank_output
    )
    base_arrived, shrink_arrived = (
        lax.all_to_all(base_terms, ("dp", "sub"), split_axis=0, concat_axis=0, tiled=True),
        lax.all_to_all(shrink_terms, ("dp", "sub"), split_axis=0, concat_axis=0, tiled=True),
    )
    frozen_sum = jnp.sum(base_arrived.astype(jnp.float32), axis=0)
    shrink = jnp.sum(shrink_arrived.astype(jnp.float32), axis=0)
    shrink_low = shrink.astype(jnp.bfloat16)
    my_ids = lax.dynamic_slice_in_dim(ids_all, group_index * group_rows, group_rows, 0)
    capacity = 2 * group_rows // adapters
    member_int = (my_ids[:, None] == catalog[None, :]).astype(jnp.int32)
    before = jnp.cumsum(member_int, axis=0) - member_int
    slot_index = jnp.sum(before * member_int, axis=1)
    position = my_ids * capacity + slot_index
    placing = (
        position[None, :] == jnp.arange(adapters * capacity, dtype=jnp.int32)[:, None]
    ).astype(jnp.bfloat16)
    outgoing = (
        jnp.dot(placing, shrink_low, preferred_element_type=jnp.float32)
        .astype(jnp.bfloat16)
        .reshape(adapters, capacity, reduced_rank_output)
    )
    received = lax.all_to_all(outgoing, ("dp", "sub"), split_axis=0, concat_axis=0, tiled=True)
    slot_count = received.shape[1]
    grid_rank = received.reshape(group_count, local_up_maps, slot_count, reduced_rank_output)
    expanded = jnp.einsum(
        "gjcr,jrf->gjcf", grid_rank, adapter_up_maps, preferred_element_type=jnp.float32
    ).astype(jnp.bfloat16)
    returned = lax.all_to_all(
        expanded.reshape(group_count * local_up_maps, slot_count, columns),
        ("dp", "sub"),
        split_axis=0,
        concat_axis=0,
        tiled=True,
    )
    returned, arrived = (returned, received)
    widen_rows = jnp.dot(
        placing.T,
        returned.reshape(adapters * capacity, columns),
        preferred_element_type=jnp.float32,
    ).astype(jnp.bfloat16)
    policy_scores = frozen_sum + adapter_scale * widen_rows.astype(jnp.float32)
    read_float = readout.astype(jnp.float32)
    score_policy, score_base = lax.psum(
        (
            jnp.sum(read_float * jax.nn.silu(policy_scores), axis=1),
            jnp.sum(read_float * jax.nn.silu(frozen_sum), axis=1),
        ),
        "tensor",
    )
    margin_rows = score_policy - score_base
    row_number = jnp.arange(group_rows, dtype=jnp.int32)
    pick_chosen = (preference_pair_rows[:, 0:1] == row_number[None, :]).astype(jnp.float32)
    pick_rejected = (preference_pair_rows[:, 1:2] == row_number[None, :]).astype(jnp.float32)
    margin = beta_pref * (
        jnp.sum(pick_chosen * margin_rows[None, :], axis=1)
        - jnp.sum(pick_rejected * margin_rows[None, :], axis=1)
    )
    weight = beta_pref * jax.nn.sigmoid(-margin)
    row_grad = jnp.sum((pick_rejected - pick_chosen) * weight[:, None], axis=0)
    output_gradient = (row_grad[:, None] * read_float * swish_slope(policy_scores)).astype(
        jnp.bfloat16
    )
    outgoing_grad = (
        jnp.dot(placing, output_gradient, preferred_element_type=jnp.float32)
        .astype(jnp.bfloat16)
        .reshape(adapters, capacity, columns)
    )
    arrived_grad = lax.all_to_all(
        outgoing_grad, ("dp", "sub"), split_axis=0, concat_axis=0, tiled=True
    )
    grid_rank = arrived.reshape(group_count, local_up_maps, capacity, reduced_rank_output)
    grid_grad = arrived_grad.reshape(group_count, local_up_maps, capacity, columns)
    up_gradient = adapter_scale * jnp.einsum(
        "gjcr,gjcf->jrf", grid_rank, grid_grad, preferred_element_type=jnp.float32
    )
    rank_slots = jnp.einsum(
        "gjcf,jrf->gjcr", grid_grad, adapter_up_maps, preferred_element_type=jnp.float32
    )
    rank_back = lax.all_to_all(
        rank_slots.reshape(group_count * local_up_maps, capacity, reduced_rank_output).astype(
            jnp.bfloat16
        ),
        ("dp", "sub"),
        split_axis=0,
        concat_axis=0,
        tiled=True,
    ).astype(jnp.float32)
    rank_portion = jnp.dot(
        placing.astype(jnp.float32).T,
        rank_back.reshape(adapters * capacity, reduced_rank_output),
        precision=lax.Precision.HIGHEST,
    )
    rank_gradient = (adapter_scale * lax.psum(rank_portion, "tensor")).astype(jnp.bfloat16)
    rank_all = lax.all_gather(rank_gradient, ("dp", "sub"), axis=0, tiled=True)
    spread_back = (member_mine[:, :, None] * rank_all.astype(jnp.float32)[:, None, :]).astype(
        jnp.bfloat16
    )
    down_gradient = jnp.einsum(
        "rd,rjk->jdk", rows_all, spread_back, preferred_element_type=jnp.float32
    )
    updated_down_maps, updated_down_first, updated_down_second = moment_update_step(
        adapter_down_maps, down_first_moment, down_second_moment, down_gradient
    )
    updated_up_maps, updated_up_first, updated_up_second = moment_update_step(
        adapter_up_maps, up_first_moment, up_second_moment, up_gradient
    )
    return (
        updated_down_maps,
        updated_down_first,
        updated_down_second,
        updated_up_maps,
        updated_up_first,
        updated_up_second,
    )


def to_device(dp, t, s):
    return {"dp": dp, "tensor": t, "sub": s}


def remote(src, dst, send_sem, recv_sem, device):
    return pltpu.make_async_remote_copy(
        src_ref=src,
        dst_ref=dst,
        send_sem=send_sem,
        recv_sem=recv_sem,
        device_id=device,
        device_id_type=pl.DeviceIdType.MESH,
    )


def rows_at(start, size):
    return pl.ds(pl.multiple_of(start, size), size)


def step_kernel(
    T, chunk, acts, w, down, up, readout, ids, pairs,
    upg, rank_out, acts_out,
    acts_all, wbuf, own, sib_out, sib_in, x_out, x_in, upbuf, rd,
    terms, terms_in, shrink_own, shrink_half, scat, pick,
    margin_own, margin_in, grad_out, ug_own, ug_out, ug_in, gx_out, gx_in, gown,
    rank_part, rank_in, rank_own, rank_all, rank_acc, score_acc,
    acts_ss, acts_rs, w_sem, local_sem, sib_ss, sib_rs, x_ss, x_rs,
    mat_ss, mat_rs, terms_ss, terms_rs, shrink_ss, shrink_rs, margin_ss, margin_rs,
    ug_ss, ug_rs, gx_ss, gx_rs, out_sem, rank_ss, rank_rs, all_ss, all_rs,
):
    dp, t, s = lax.axis_index("dp"), lax.axis_index("tensor"), lax.axis_index("sub")
    rows = acts_all.shape[0]
    half = rows // 2
    group = half // 2
    columns = w.shape[1]
    span = columns // 2
    chunks = span // chunk
    rank = down.shape[1]
    share = half // (2 * T)
    M = 2 * T
    mine = dp * T + t
    me = mine * 2 + s
    sibling = to_device(dp, t, 1 - s)
    across = to_device(1 - dp, t, s)
    here = pl.multiple_of(dp * span, 128)
    there = pl.multiple_of((1 - dp) * span, 128)

    def w_copy(c):
        base = jnp.where(c < chunks, 1 - dp, dp) * span
        off = base + lax.rem(c, chunks) * chunk
        return pltpu.make_async_copy(
            w.at[:, pl.ds(pl.multiple_of(off, 128), chunk)], wbuf.at[c], w_sem.at[c]
        )

    def device_at(k):
        number = lax.rem(me + k, 2 * M)
        return number, number // (2 * T), lax.rem(number // 2, T), lax.rem(number, 2)

    @pl.loop(0, 2)
    def _(c):
        w_copy(c).start()

    up_local = pltpu.make_async_copy(up.at[:, pl.ds(here, span)], upbuf.at[0:group], local_sem.at[0])
    rd_local = pltpu.make_async_copy(
        readout.at[:, pl.ds(here, span)], rd.at[rows_at(dp * group, group)], local_sem.at[1]
    )
    own_slot = rows_at((lax.rem(t + s, 2) * 2 + t // 2) * group, group)
    acts_local = pltpu.make_async_copy(acts, acts_all.at[own_slot], local_sem.at[2])
    up_local.start()
    rd_local.start()
    acts_local.start()

    barrier = pltpu.get_barrier_semaphore()

    @pl.loop(1, 2 * M)
    def _(k):
        _, d, z, c = device_at(k)
        pl.semaphore_signal(
            barrier, inc=1, device_id=to_device(d, z, c), device_id_type=pl.DeviceIdType.MESH
        )

    pl.semaphore_wait(barrier, 2 * M - 1)

    def acts_copy(k):
        return remote(
            acts, acts_all.at[own_slot], acts_ss.at[k], acts_rs.at[t], to_device(dp, lax.rem(t + k, T), s)
        )

    def acts_arrival(k):
        z = lax.rem(t + k, T)
        slot = rows_at((lax.rem(z + s, 2) * 2 + z // 2) * group, group)
        return remote(acts, acts_all.at[slot], acts_ss.at[k], acts_rs.at[z], across)

    @pl.loop(1, T)
    def _(k):
        acts_copy(k).start()

    up_across = remote(
        up.at[:, pl.ds(there, span)], upbuf.at[group : 2 * group], mat_ss.at[0], mat_rs.at[0], across
    )
    up_beside = remote(
        up.at[:, pl.ds(here, span)], upbuf.at[2 * group : 3 * group], mat_ss.at[1], mat_rs.at[1], sibling
    )
    up_forward = remote(
        upbuf.at[group : 2 * group], upbuf.at[3 * group : 4 * group], mat_ss.at[2], mat_rs.at[2], sibling
    )
    rd_across = remote(
        readout.at[:, pl.ds(there, span)],
        rd.at[rows_at(dp * group, group)],
        mat_ss.at[3],
        mat_rs.at[3],
        across,
    )
    row_lane = lax.broadcasted_iota(jnp.int32, (pairs.shape[0], half), 1) - dp * group
    pick[dp] = (pairs[:, 0:1] == row_lane).astype(jnp.float32) - (
        pairs[:, 1:2] == row_lane
    ).astype(jnp.float32)
    pick_across = remote(pick.at[dp], pick.at[dp], mat_ss.at[4], mat_rs.at[4], across)
    pick_arrival = remote(pick.at[1 - dp], pick.at[1 - dp], mat_ss.at[4], mat_rs.at[4], across)
    rd_arrival = remote(
        readout.at[:, pl.ds(there, span)],
        rd.at[rows_at((1 - dp) * group, group)],
        mat_ss.at[3],
        mat_rs.at[3],
        across,
    )
    up_across.start()
    rd_across.start()
    pick_across.start()
    up_beside.start()

    @pl.loop(2, 2 * chunks)
    def _(c):
        w_copy(c).start()

    acts_local.wait()

    @pl.loop(1, T)
    def _(k):
        acts_arrival(k).wait_recv()

    acts_back = pltpu.make_async_copy(acts_all, acts_out, local_sem.at[3])
    acts_back.start()

    first = [ids[g * group : (g + 1) * group] for g in range(4)]
    ids_even = jnp.concatenate([first[0], first[2]], axis=0)
    ids_odd = jnp.concatenate([first[1], first[3]], axis=0)
    on_odd = jnp.full((half, 1), s, jnp.int32) == 1
    ids_own = jnp.where(on_odd, ids_odd, ids_even)
    ids_sib = jnp.where(on_odd, ids_even, ids_odd)
    ids_all = jnp.concatenate([ids_own, ids_sib], axis=0)

    products = jnp.dot(acts_all[...], down[...], preferred_element_type=jnp.float32)
    terms[...] = jnp.where(ids_all == t, products, 0.0).astype(jnp.bfloat16)

    def terms_copy(k):
        number, d, z, c = device_at(k)
        block = jnp.where(c == s, 0, M) + d * T + z
        return remote(
            terms.at[rows_at(block * share, share)],
            terms_in.at[me],
            terms_ss.at[number],
            terms_rs.at[me],
            to_device(d, z, c),
        )

    def terms_arrival(k):
        number, d, z, c = device_at(k)
        return remote(
            terms.at[0:share], terms_in.at[number], terms_ss.at[number], terms_rs.at[number], sibling
        )

    def same_sub(k):
        number = lax.rem(mine + k, M)
        return number, number // T, lax.rem(number, T)

    def shrink_copy(k):
        number, d, z = same_sub(k)
        return remote(
            shrink_own,
            shrink_half.at[rows_at(mine * share, share)],
            shrink_ss.at[number],
            shrink_rs.at[mine],
            to_device(d, z, s),
        )

    def shrink_arrival(k):
        number, d, z = same_sub(k)
        return remote(
            shrink_own,
            shrink_half.at[rows_at(number * share, share)],
            shrink_ss.at[number],
            shrink_rs.at[number],
            sibling,
        )

    @pl.loop(1, 2 * M)
    def _(k):
        terms_copy(k).start()

    terms_in[me] = terms[rows_at(mine * share, share)]

    def sib_copy(c):
        return remote(sib_out.at[c], sib_in.at[c], sib_ss.at[c], sib_rs.at[c], sibling)

    def x_copy(c):
        return remote(x_out.at[c], x_in.at[c], x_ss.at[c], x_rs.at[c], across)

    def add_sibling(c):
        sib_copy(c).wait_recv()
        total = own[c] + sib_in[c].astype(jnp.float32)

        @pl.when(c < chunks)
        def _():
            x_out[jnp.minimum(c, chunks - 1)] = total.astype(jnp.bfloat16)
            x_copy(jnp.minimum(c, chunks - 1)).start()

        @pl.when(c >= chunks)
        def _():
            own[c] = total

    @pl.loop(0, 2 * chunks)
    def _(c):
        w_copy(c).wait()
        part = jnp.dot(acts_all[...], wbuf[c], preferred_element_type=jnp.float32)
        sib_out[c] = part[half:].astype(jnp.bfloat16)
        sib_copy(c).start()
        own[c] = part[:half].astype(jnp.bfloat16).astype(jnp.float32)

        @pl.when(c > 0)
        def _():
            add_sibling(c - 1)

        @pl.when(c == 2)
        def _():
            @pl.loop(1, 2 * M)
            def _(k):
                terms_arrival(k).wait_recv()

            low = jnp.sum(terms_in[...].astype(jnp.float32), axis=0).astype(jnp.bfloat16)
            shrink_own[...] = low
            shrink_half[rows_at(mine * share, share)] = low

            @pl.loop(1, M)
            def _(k):
                shrink_copy(k).start()

    add_sibling(2 * chunks - 1)
    up_across.wait_recv()
    up_forward.start()

    @pl.loop(1, M)
    def _(k):
        shrink_arrival(k).wait_recv()

    slot_own = (ids_own + s) % 2 * 2 + (ids_own // 2 + dp) % 2
    low = shrink_half[...]
    lane_slot = lax.broadcasted_iota(jnp.int32, (half, 4 * rank), 1) // rank
    scat[...] = jnp.where(
        slot_own == lane_slot, jnp.concatenate([low] * 4, axis=1).astype(jnp.float32), 0.0
    ).astype(jnp.bfloat16)
    up_local.wait()
    rd_local.wait()
    up_beside.wait_recv()
    rd_arrival.wait_recv()
    up_forward.wait_recv()
    score_acc[...] = jnp.zeros_like(score_acc)

    def columns_of(j):
        return pl.ds(pl.multiple_of(j * chunk, 128), chunk)

    @pl.loop(0, chunks)
    def _(j):
        x_copy(j).wait_recv()
        base = own[chunks + j] + x_in[j].astype(jnp.float32)
        widened = jnp.dot(
            scat[...], upbuf[:, columns_of(j)], preferred_element_type=jnp.float32
        ).astype(jnp.bfloat16)
        policy = base + adapter_scale * widened.astype(jnp.float32)
        read = rd[:, columns_of(j)].astype(jnp.float32)
        sig = jax.nn.sigmoid(policy)
        gain = read * (policy * sig - base * jax.nn.sigmoid(base))
        total = score_acc[...]
        for i in range(chunk // 128):
            total = total + gain[:, i * 128 : (i + 1) * 128]
        score_acc[...] = total
        own[chunks + j] = read * (sig * (1.0 + policy * (1.0 - sig)))

    margin_own[...] = jnp.broadcast_to(
        jnp.sum(score_acc[...].T, axis=0, keepdims=True), margin_own.shape
    )

    def margin_copy(k):
        number, d, z = same_sub(k)
        return remote(
            margin_own, margin_in.at[mine], margin_ss.at[number], margin_rs.at[mine], to_device(d, z, s)
        )

    def margin_arrival(k):
        number, d, z = same_sub(k)
        return remote(
            margin_own, margin_in.at[number], margin_ss.at[number], margin_rs.at[number], sibling
        )

    @pl.loop(1, M)
    def _(k):
        margin_copy(k).start()

    margin_in[mine] = margin_own[...]
    pick_arrival.wait_recv()

    @pl.loop(1, M)
    def _(k):
        margin_arrival(k).wait_recv()

    margin_rows = jnp.sum(margin_in[...], axis=0)[0:1]
    picks = pick[...].reshape(-1, half)
    margin = beta_pref * jnp.sum(picks * margin_rows, axis=1, keepdims=True)
    weight = beta_pref * jax.nn.sigmoid(-margin)
    row_grad = -jnp.sum(picks * weight, axis=0, keepdims=True)
    row_column = jnp.broadcast_to(row_grad, (half, half)).T[:, 0:1]
    rank_acc[...] = jnp.zeros_like(rank_acc)

    def ug_copy(j):
        return remote(ug_out.at[j], ug_in.at[j], ug_ss.at[j], ug_rs.at[j], sibling)

    def gx_copy(j):
        return remote(gx_out.at[j], gx_in.at[j], gx_ss.at[j], gx_rs.at[j], across)

    def out_copy(j):
        off = pl.multiple_of(dp * span + j * chunk, 128)
        return pltpu.make_async_copy(gown.at[j], upg.at[:, pl.ds(off, chunk)], out_sem.at[j])

    def out_copy_across(j):
        off = pl.multiple_of((1 - dp) * span + j * chunk, 128)
        return pltpu.make_async_copy(
            gx_in.at[j], upg.at[:, pl.ds(off, chunk)], out_sem.at[chunks + j]
        )

    def add_up(j):
        ug_copy(j).wait_recv()
        total = (ug_own[j] + ug_in[j].astype(jnp.float32)).astype(jnp.bfloat16)
        gx_out[j] = total[group:]
        gx_copy(j).start()
        gown[j] = total[:group]
        out_copy(j).start()

    @pl.loop(0, chunks)
    def _(j):
        grad = (row_column * own[chunks + j]).astype(jnp.bfloat16)
        ug = lax.dot_general(
            scat[...], grad, (((0,), (0,)), ((), ())), preferred_element_type=jnp.float32
        )
        ug = adapter_scale * ug
        ug_out[j] = ug[half:].astype(jnp.bfloat16)
        ug_copy(j).start()
        ug_own[j] = ug[:half]
        rank_acc[...] += lax.dot_general(
            grad,
            upbuf[:, columns_of(j)],
            (((1,), (1,)), ((), ())),
            preferred_element_type=jnp.float32,
        )

        @pl.when(j > 0)
        def _():
            add_up(j - 1)

    every = jnp.where(slot_own == lane_slot, rank_acc[...], 0.0)
    rank_part[...] = sum(every[:, i * rank : (i + 1) * rank] for i in range(4))

    def rank_copy(k):
        number, d, z = same_sub(k)
        return remote(
            rank_part.at[rows_at(number * share, share)],
            rank_in.at[mine],
            rank_ss.at[number],
            rank_rs.at[mine],
            to_device(d, z, s),
        )

    def rank_arrival(k):
        number, d, z = same_sub(k)
        return remote(
            rank_part.at[0:share], rank_in.at[number], rank_ss.at[number], rank_rs.at[number], sibling
        )

    @pl.loop(1, M)
    def _(k):
        rank_copy(k).start()

    rank_in[mine] = rank_part[rows_at(mine * share, share)]
    add_up(chunks - 1)

    @pl.loop(1, M)
    def _(k):
        rank_arrival(k).wait_recv()

    low = (adapter_scale * jnp.sum(rank_in[...], axis=0)).astype(jnp.bfloat16)
    rank_own[...] = low

    def all_copy(k):
        number, d, z, c = device_at(k)
        block = jnp.where(c == s, 0, M) + mine
        return remote(
            rank_own,
            rank_all.at[rows_at(block * share, share)],
            all_ss.at[number],
            all_rs.at[me],
            to_device(d, z, c),
        )

    def all_arrival(k):
        number, d, z, c = device_at(k)
        block = jnp.where(c == s, 0, M) + d * T + z
        return remote(
            rank_own,
            rank_all.at[rows_at(block * share, share)],
            all_ss.at[number],
            all_rs.at[number],
            sibling,
        )

    @pl.loop(1, 2 * M)
    def _(k):
        all_copy(k).start()

    rank_all[rows_at(mine * share, share)] = low

    @pl.loop(1, 2 * M)
    def _(k):
        all_arrival(k).wait_recv()

    rank_out[...] = jnp.where(ids_all == t, rank_all[...].astype(jnp.float32), 0.0).astype(
        jnp.bfloat16
    )

    @pl.loop(0, chunks)
    def _(j):
        gx_copy(j).wait_recv()
        out_copy_across(j).start()

    @pl.loop(0, chunks)
    def _(j):
        x_copy(j).wait_send()
        ug_copy(j).wait_send()
        gx_copy(j).wait_send()
        out_copy(j).wait()
        out_copy_across(j).wait()

    @pl.loop(0, 2 * chunks)
    def _(c):
        sib_copy(c).wait_send()

    @pl.loop(1, T)
    def _(k):
        acts_copy(k).wait_send()

    @pl.loop(1, M)
    def _(k):
        shrink_copy(k).wait_send()
        margin_copy(k).wait_send()
        rank_copy(k).wait_send()

    @pl.loop(1, 2 * M)
    def _(k):
        terms_copy(k).wait_send()
        all_copy(k).wait_send()

    up_across.wait_send()
    up_beside.wait_send()
    up_forward.wait_send()
    rd_across.wait_send()
    pick_across.wait_send()
    acts_back.wait()


def fast_body(
    acts,
    frozen_weight,
    adapter_down_maps,
    adapter_up_maps,
    down_first_moment,
    down_second_moment,
    up_first_moment,
    up_second_moment,
    readout,
    adapter_index_rows,
    preference_pair_rows,
):
    T = lax.axis_size("tensor")
    group, depth = acts.shape
    rows = T * group
    half = rows // 2
    columns = frozen_weight.shape[1]
    span = columns // 2
    rank = adapter_down_maps.shape[2]
    chunk = chunk_of(span)
    chunks = span // chunk
    M = 2 * T
    share = half // M
    bf16, f32 = jnp.bfloat16, jnp.float32
    V, dma = pltpu.VMEM, pltpu.SemaphoreType.DMA
    any_spec = pl.BlockSpec(memory_space=pl.ANY)
    vmem_spec = pl.BlockSpec(memory_space=pltpu.VMEM)
    up_grad, rank_masked, rows_all = pl.pallas_call(
        functools.partial(step_kernel, T, chunk),
        out_shape=(
            jax.ShapeDtypeStruct((rank, columns), bf16),
            jax.ShapeDtypeStruct((rows, rank), bf16),
            jax.ShapeDtypeStruct((rows, depth), bf16),
        ),
        in_specs=[vmem_spec, any_spec, vmem_spec, any_spec, any_spec, vmem_spec, vmem_spec],
        out_specs=(any_spec, vmem_spec, any_spec),
        scratch_shapes=[
            V((rows, depth), bf16),
            V((2 * chunks, depth, chunk), bf16),
            V((2 * chunks, half, chunk), f32),
            V((2 * chunks, half, chunk), bf16),
            V((2 * chunks, half, chunk), bf16),
            V((chunks, half, chunk), bf16),
            V((chunks, half, chunk), bf16),
            V((4 * rank, span), bf16),
            V((half, span), bf16),
            V((rows, rank), bf16),
            V((2 * M, share, rank), bf16),
            V((share, rank), bf16),
            V((half, rank), bf16),
            V((half, 4 * rank), bf16),
            V((2, group // 2, half), f32),
            V((8, half), f32),
            V((M, 8, half), f32),
            V((8, 128), f32),
            V((chunks, half, chunk), f32),
            V((chunks, half, chunk), bf16),
            V((chunks, half, chunk), bf16),
            V((chunks, group, chunk), bf16),
            V((chunks, group, chunk), bf16),
            V((chunks, group, chunk), bf16),
            V((half, rank), f32),
            V((M, share, rank), f32),
            V((share, rank), bf16),
            V((rows, rank), bf16),
            V((half, 4 * rank), f32),
            V((half, 128), f32),
            dma((T,)), dma((T,)), dma((2 * chunks,)), dma((4,)),
            dma((2 * chunks,)), dma((2 * chunks,)), dma((chunks,)), dma((chunks,)),
            dma((5,)), dma((5,)), dma((2 * M,)), dma((2 * M,)),
            dma((M,)), dma((M,)), dma((M,)), dma((M,)),
            dma((chunks,)), dma((chunks,)), dma((chunks,)), dma((chunks,)),
            dma((2 * chunks,)), dma((M,)), dma((M,)), dma((2 * M,)), dma((2 * M,)),
        ],
        compiler_params=pltpu.CompilerParams(
            collective_id=0, has_side_effects=True, vmem_limit_bytes=52 * 1024 * 1024
        ),
    )(
        acts,
        frozen_weight,
        adapter_down_maps[0],
        adapter_up_maps[0],
        readout,
        adapter_index_rows,
        preference_pair_rows,
    )
    down_gradient = jnp.einsum("rd,rk->dk", rows_all, rank_masked, preferred_element_type=f32)[None]
    up_gradient = up_grad.astype(f32)[None]
    return moment_update_step(
        adapter_down_maps, down_first_moment, down_second_moment, down_gradient
    ) + moment_update_step(adapter_up_maps, up_first_moment, up_second_moment, up_gradient)


def chunk_of(span):
    return next((c for c in (640, 512, 384, 256, 128) if span % c == 0), 0)


def fits(mesh, args):
    sizes = mesh.shape
    T = sizes["tensor"]
    if sizes["dp"] != 2 or sizes["sub"] != 2 or T != 4:
        return False
    rows = args[0].shape[0] // sizes["parts"]
    span = args[1].shape[1] // (2 * T)
    rank = args[2].shape[2]
    return rows == 256 and rank == 64 and args[2].shape[0] == 4 * sizes["parts"] and chunk_of(span) > 0


def solution(mesh):
    placed = (
        P(("parts", "tensor"), ("dp", "sub")),
        P(("dp", "sub"), "tensor"),
        P(("parts", "tensor"), ("dp", "sub"), None),
        P(("parts", "dp", "sub"), None, "tensor"),
        P(("parts", "tensor"), ("dp", "sub"), None),
        P(("parts", "tensor"), ("dp", "sub"), None),
        P(("parts", "dp", "sub"), None, "tensor"),
        P(("parts", "dp", "sub"), None, "tensor"),
        P(("parts", "dp", "sub"), "tensor"),
        P("parts", None),
        P(("parts", "dp", "sub"), None),
    )
    def run(*args):
        return sharded(fast_body if fits(mesh, args) else body)(*args)

    sharded = lambda inner: jax.shard_map(
        inner,
        mesh=mesh,
        in_specs=placed,
        out_specs=(
            P(("parts", "tensor"), ("dp", "sub"), None),
            P(("parts", "tensor"), ("dp", "sub"), None),
            P(("parts", "tensor"), ("dp", "sub"), None),
            P(("parts", "dp", "sub"), None, "tensor"),
            P(("parts", "dp", "sub"), None, "tensor"),
            P(("parts", "dp", "sub"), None, "tensor"),
        ),
        check_vma=False,
    )
    return run
```

```python
import functools

import jax
import jax.numpy as jnp
from jax import lax
from jax.experimental import pallas as pl
from jax.experimental.pallas import tpu as pltpu
from jax.sharding import PartitionSpec as P

adapter_scale = 2.0
beta_pref = 0.1
learn_rate = 0.001
first_decay = 0.9
second_decay = 0.95
first_fix = 1.0 - 2.656139888758747e-05
second_fix = 1.0 - 0.005920529220334
adam_eps = 1e-08


def swish_slope(pre_act):
    sigmoid_of = jax.nn.sigmoid(pre_act)
    return sigmoid_of * (1.0 + pre_act * (1.0 - sigmoid_of))


def moment_update_step(param, mean_old, square_old, grad):
    new_mean = first_decay * mean_old + (1.0 - first_decay) * grad
    new_square = second_decay * square_old + (1.0 - second_decay) * grad * grad
    update_step = new_mean / first_fix / (jnp.sqrt(new_square / second_fix) + adam_eps)
    new_param = (param.astype(jnp.float32) - learn_rate * update_step).astype(jnp.bfloat16)
    return (new_param, new_mean, new_square)


def body(
    acts,
    frozen_weight,
    adapter_down_maps,
    adapter_up_maps,
    down_first_moment,
    down_second_moment,
    up_first_moment,
    up_second_moment,
    readout,
    adapter_index_rows,
    preference_pair_rows,
):
    group_count = lax.axis_size(("dp", "sub"))
    group_index = lax.axis_index(("dp", "sub"))
    tensor_index = lax.axis_index("tensor")
    reduced_rank_output = adapter_down_maps.shape[2]
    local_down_maps = adapter_down_maps.shape[0]
    local_up_maps = adapter_up_maps.shape[0]
    adapters = local_up_maps * group_count
    group_rows = readout.shape[0]
    columns = readout.shape[1]
    ids_all = adapter_index_rows[:, 0]
    catalog = jnp.arange(adapters, dtype=jnp.int32)
    member_all = (ids_all[:, None] == catalog[None, :]).astype(jnp.float32)
    member_mine = lax.dynamic_slice_in_dim(
        member_all, tensor_index * local_down_maps, local_down_maps, 1
    )
    rows_all = lax.all_gather(acts, "tensor", axis=0, tiled=True)
    base_part = jnp.dot(rows_all, frozen_weight, preferred_element_type=jnp.float32)
    down_maps_total = lax.all_gather(adapter_down_maps, "tensor", axis=0, tiled=True)
    products = jnp.einsum(
        "rd,adk->rak", rows_all, down_maps_total, preferred_element_type=jnp.float32
    )
    shrink_part = jnp.sum(products * member_all[:, :, None], axis=1)
    base_terms = base_part.astype(jnp.bfloat16).reshape(group_count, group_rows, columns)
    shrink_terms = shrink_part.astype(jnp.bfloat16).reshape(
        group_count, group_rows, reduced_rank_output
    )
    base_arrived, shrink_arrived = (
        lax.all_to_all(base_terms, ("dp", "sub"), split_axis=0, concat_axis=0, tiled=True),
        lax.all_to_all(shrink_terms, ("dp", "sub"), split_axis=0, concat_axis=0, tiled=True),
    )
    frozen_sum = jnp.sum(base_arrived.astype(jnp.float32), axis=0)
    shrink = jnp.sum(shrink_arrived.astype(jnp.float32), axis=0)
    shrink_low = shrink.astype(jnp.bfloat16)
    my_ids = lax.dynamic_slice_in_dim(ids_all, group_index * group_rows, group_rows, 0)
    capacity = 2 * group_rows // adapters
    member_int = (my_ids[:, None] == catalog[None, :]).astype(jnp.int32)
    before = jnp.cumsum(member_int, axis=0) - member_int
    slot_index = jnp.sum(before * member_int, axis=1)
    position = my_ids * capacity + slot_index
    placing = (
        position[None, :] == jnp.arange(adapters * capacity, dtype=jnp.int32)[:, None]
    ).astype(jnp.bfloat16)
    outgoing = (
        jnp.dot(placing, shrink_low, preferred_element_type=jnp.float32)
        .astype(jnp.bfloat16)
        .reshape(adapters, capacity, reduced_rank_output)
    )
    received = lax.all_to_all(outgoing, ("dp", "sub"), split_axis=0, concat_axis=0, tiled=True)
    slot_count = received.shape[1]
    grid_rank = received.reshape(group_count, local_up_maps, slot_count, reduced_rank_output)
    expanded = jnp.einsum(
        "gjcr,jrf->gjcf", grid_rank, adapter_up_maps, preferred_element_type=jnp.float32
    ).astype(jnp.bfloat16)
    returned = lax.all_to_all(
        expanded.reshape(group_count * local_up_maps, slot_count, columns),
        ("dp", "sub"),
        split_axis=0,
        concat_axis=0,
        tiled=True,
    )
    returned, arrived = (returned, received)
    widen_rows = jnp.dot(
        placing.T,
        returned.reshape(adapters * capacity, columns),
        preferred_element_type=jnp.float32,
    ).astype(jnp.bfloat16)
    policy_scores = frozen_sum + adapter_scale * widen_rows.astype(jnp.float32)
    read_float = readout.astype(jnp.float32)
    score_policy, score_base = lax.psum(
        (
            jnp.sum(read_float * jax.nn.silu(policy_scores), axis=1),
            jnp.sum(read_float * jax.nn.silu(frozen_sum), axis=1),
        ),
        "tensor",
    )
    margin_rows = score_policy - score_base
    row_number = jnp.arange(group_rows, dtype=jnp.int32)
    pick_chosen = (preference_pair_rows[:, 0:1] == row_number[None, :]).astype(jnp.float32)
    pick_rejected = (preference_pair_rows[:, 1:2] == row_number[None, :]).astype(jnp.float32)
    margin = beta_pref * (
        jnp.sum(pick_chosen * margin_rows[None, :], axis=1)
        - jnp.sum(pick_rejected * margin_rows[None, :], axis=1)
    )
    weight = beta_pref * jax.nn.sigmoid(-margin)
    row_grad = jnp.sum((pick_rejected - pick_chosen) * weight[:, None], axis=0)
    output_gradient = (row_grad[:, None] * read_float * swish_slope(policy_scores)).astype(
        jnp.bfloat16
    )
    outgoing_grad = (
        jnp.dot(placing, output_gradient, preferred_element_type=jnp.float32)
        .astype(jnp.bfloat16)
        .reshape(adapters, capacity, columns)
    )
    arrived_grad = lax.all_to_all(
        outgoing_grad, ("dp", "sub"), split_axis=0, concat_axis=0, tiled=True
    )
    grid_rank = arrived.reshape(group_count, local_up_maps, capacity, reduced_rank_output)
    grid_grad = arrived_grad.reshape(group_count, local_up_maps, capacity, columns)
    up_gradient = adapter_scale * jnp.einsum(
        "gjcr,gjcf->jrf", grid_rank, grid_grad, preferred_element_type=jnp.float32
    )
    rank_slots = jnp.einsum(
        "gjcf,jrf->gjcr", grid_grad, adapter_up_maps, preferred_element_type=jnp.float32
    )
    rank_back = lax.all_to_all(
        rank_slots.reshape(group_count * local_up_maps, capacity, reduced_rank_output).astype(
            jnp.bfloat16
        ),
        ("dp", "sub"),
        split_axis=0,
        concat_axis=0,
        tiled=True,
    ).astype(jnp.float32)
    rank_portion = jnp.dot(
        placing.astype(jnp.float32).T,
        rank_back.reshape(adapters * capacity, reduced_rank_output),
        precision=lax.Precision.HIGHEST,
    )
    rank_gradient = (adapter_scale * lax.psum(rank_portion, "tensor")).astype(jnp.bfloat16)
    rank_all = lax.all_gather(rank_gradient, ("dp", "sub"), axis=0, tiled=True)
    spread_back = (member_mine[:, :, None] * rank_all.astype(jnp.float32)[:, None, :]).astype(
        jnp.bfloat16
    )
    down_gradient = jnp.einsum(
        "rd,rjk->jdk", rows_all, spread_back, preferred_element_type=jnp.float32
    )
    updated_down_maps, updated_down_first, updated_down_second = moment_update_step(
        adapter_down_maps, down_first_moment, down_second_moment, down_gradient
    )
    updated_up_maps, updated_up_first, updated_up_second = moment_update_step(
        adapter_up_maps, up_first_moment, up_second_moment, up_gradient
    )
    return (
        updated_down_maps,
        updated_down_first,
        updated_down_second,
        updated_up_maps,
        updated_up_first,
        updated_up_second,
    )


def to_device(dp, t, s):
    return {"dp": dp, "tensor": t, "sub": s}


def remote(src, dst, send_sem, recv_sem, device):
    return pltpu.make_async_remote_copy(
        src_ref=src,
        dst_ref=dst,
        send_sem=send_sem,
        recv_sem=recv_sem,
        device_id=device,
        device_id_type=pl.DeviceIdType.MESH,
    )


def rows_at(start, size):
    return pl.ds(pl.multiple_of(start, size), size)


def step_kernel(
    T, chunk, acts, w, down_in, up, readout, ids_in, pairs_in,
    upg, rank_out, acts_out,
    acts_all, wbuf, own, sib_out, sib_in, x_out, x_in, upbuf, rd,
    terms, terms_in, shrink_own, shrink_half, scat, pick,
    margin_own, margin_in, grad_out, ug_own, ug_out, ug_in, gx_out, gx_in, gown,
    rank_part, rank_in, rank_own, rank_all, rank_acc, score_acc, down, ids, pairs, grads,
    acts_ss, acts_rs, w_sem, local_sem, sib_ss, sib_rs, x_ss, x_rs,
    mat_ss, mat_rs, terms_ss, terms_rs, shrink_ss, shrink_rs, margin_ss, margin_rs,
    ug_ss, ug_rs, gx_ss, gx_rs, out_sem, rank_ss, rank_rs, all_ss, all_rs,
):
    dp, t, s = lax.axis_index("dp"), lax.axis_index("tensor"), lax.axis_index("sub")
    rows = acts_all.shape[0]
    half = rows // 2
    group = half // 2
    columns = w.shape[1]
    span = columns // 2
    chunks = span // chunk
    rank = down.shape[0]
    share = half // T
    M = 2 * T
    mine = dp * T + t
    me = mine * 2 + s
    sibling = to_device(dp, t, 1 - s)
    across = to_device(1 - dp, t, s)
    here = pl.multiple_of(dp * span, 128)
    there = pl.multiple_of((1 - dp) * span, 128)

    def w_copy(c):
        base = jnp.where(c < chunks, 1 - dp, dp) * span
        off = base + lax.rem(c, chunks) * chunk
        return pltpu.make_async_copy(
            w.at[:, pl.ds(pl.multiple_of(off, 128), chunk)], wbuf.at[c], w_sem.at[c]
        )

    def device_at(k):
        number = lax.rem(me + k, 2 * M)
        return number, number // (2 * T), lax.rem(number // 2, T), lax.rem(number, 2)

    ids_local = pltpu.make_async_copy(ids_in, ids, local_sem.at[4])
    pairs_local = pltpu.make_async_copy(pairs_in, pairs, local_sem.at[5])
    down_local = pltpu.make_async_copy(down_in, down, local_sem.at[6])
    ids_local.start()
    pairs_local.start()
    down_local.start()

    @pl.loop(0, 2)
    def _(c):
        w_copy(c).start()

    up_local = pltpu.make_async_copy(up.at[:, pl.ds(here, span)], upbuf.at[0:group], local_sem.at[0])
    rd_local = pltpu.make_async_copy(
        readout.at[:, pl.ds(here, span)], rd.at[rows_at(dp * group, group)], local_sem.at[1]
    )
    own_slot = rows_at((lax.rem(t + s, 2) * 2 + t // 2) * group, group)
    acts_local = pltpu.make_async_copy(acts, acts_all.at[own_slot], local_sem.at[2])
    up_local.start()
    rd_local.start()
    acts_local.start()

    barrier = pltpu.get_barrier_semaphore()

    @pl.loop(1, 2 * M)
    def _(k):
        _, d, z, c = device_at(k)
        pl.semaphore_signal(
            barrier, inc=1, device_id=to_device(d, z, c), device_id_type=pl.DeviceIdType.MESH
        )

    pl.semaphore_wait(barrier, 2 * M - 1)

    def acts_slot(z):
        return acts_all.at[rows_at((lax.rem(z + s, 2) * 2 + z // 2) * group, group)]

    def acts_up(i):
        block = t - i
        return remote(
            acts_slot(block), acts_slot(block), acts_ss.at[i], acts_rs.at[block], to_device(dp, t + 1, s)
        )

    def acts_downward(i):
        block = t + i
        return remote(
            acts_slot(block),
            acts_slot(block),
            acts_ss.at[T + i],
            acts_rs.at[block],
            to_device(dp, t - 1, s),
        )

    def acts_arrival(block):
        return remote(acts_slot(block), acts_slot(block), acts_ss.at[0], acts_rs.at[block], sibling)

    def when_up(i):
        return (t - i >= 0) & (t + 1 < T)

    def when_down(i):
        return (t + i < T) & (t >= 1)

    acts_local.wait()

    @pl.when(when_up(0))
    def _():
        acts_up(0).start()

    @pl.when(when_down(0))
    def _():
        acts_downward(0).start()

    up_across = remote(
        up.at[:, pl.ds(there, span)], upbuf.at[group : 2 * group], mat_ss.at[0], mat_rs.at[0], across
    )
    up_beside = remote(
        up.at[:, pl.ds(here, span)], upbuf.at[2 * group : 3 * group], mat_ss.at[1], mat_rs.at[1], sibling
    )
    up_forward = remote(
        upbuf.at[group : 2 * group], upbuf.at[3 * group : 4 * group], mat_ss.at[2], mat_rs.at[2], sibling
    )
    rd_across = remote(
        readout.at[:, pl.ds(there, span)],
        rd.at[rows_at(dp * group, group)],
        mat_ss.at[3],
        mat_rs.at[3],
        across,
    )
    pick_across = remote(pick.at[dp], pick.at[dp], mat_ss.at[4], mat_rs.at[4], across)
    pick_arrival = remote(pick.at[1 - dp], pick.at[1 - dp], mat_ss.at[4], mat_rs.at[4], across)
    rd_arrival = remote(
        readout.at[:, pl.ds(there, span)],
        rd.at[rows_at((1 - dp) * group, group)],
        mat_ss.at[3],
        mat_rs.at[3],
        across,
    )
    up_across.start()
    rd_across.start()
    up_beside.start()

    @pl.loop(2, 2 * chunks)
    def _(c):
        w_copy(c).start()

    pairs_local.wait()
    row_line = lax.broadcasted_iota(jnp.int32, (half, group // 2), 0) - dp * group
    pick[dp] = (
        (pairs[0:1] == row_line).astype(jnp.float32) - (pairs[1:2] == row_line).astype(jnp.float32)
    ).T
    pick_across.start()
    ids_local.wait()
    ids_column = jnp.broadcast_to(ids[...].astype(jnp.float32), (128, rows)).T[:, 0:1]
    ids_column = ids_column.astype(jnp.int32)
    first = [ids_column[g * group : (g + 1) * group] for g in range(4)]
    ids_even = jnp.concatenate([first[0], first[2]], axis=0)
    ids_odd = jnp.concatenate([first[1], first[3]], axis=0)
    on_odd = jnp.full((half, 1), s, jnp.int32) == 1
    ids_own = jnp.where(on_odd, ids_odd, ids_even)
    ids_sib = jnp.where(on_odd, ids_even, ids_odd)
    ids_all = jnp.concatenate([ids_own, ids_sib], axis=0)

    down_local.wait()

    @pl.loop(1, T)
    def _(i):
        @pl.when(t - i >= 0)
        def _():
            acts_arrival(t - i).wait_recv()

            @pl.when(when_up(i))
            def _():
                acts_up(i).start()

        @pl.when(t + i < T)
        def _():
            acts_arrival(t + i).wait_recv()

            @pl.when(when_down(i))
            def _():
                acts_downward(i).start()

    acts_back = pltpu.make_async_copy(acts_all, acts_out, local_sem.at[3])
    acts_back.start()
    products = lax.dot_general(
        acts_all[...], down[...], (((1,), (1,)), ((), ())), preferred_element_type=jnp.float32
    )
    terms[...] = jnp.where(ids_all == t, products, 0.0).astype(jnp.bfloat16)

    def terms_copy(k):
        number, d, z, c = device_at(k)
        block = jnp.where(c == s, 0, T) + z
        return remote(
            terms.at[rows_at(block * share, share)],
            terms_in.at[me],
            terms_ss.at[number],
            terms_rs.at[me],
            to_device(d, z, c),
        )

    def terms_arrival(k):
        number, d, z, c = device_at(k)
        return remote(
            terms.at[0:share], terms_in.at[number], terms_ss.at[number], terms_rs.at[number], sibling
        )

    def same_sub(k):
        number = lax.rem(mine + k, M)
        return number, number // T, lax.rem(number, T)

    def shrink_copy(k):
        z = lax.rem(t + k, T)
        return remote(
            shrink_own,
            shrink_half.at[rows_at(t * share, share)],
            shrink_ss.at[z],
            shrink_rs.at[t],
            to_device(dp, z, s),
        )

    def shrink_arrival(k):
        z = lax.rem(t + k, T)
        return remote(
            shrink_own,
            shrink_half.at[rows_at(z * share, share)],
            shrink_ss.at[z],
            shrink_rs.at[z],
            sibling,
        )

    @pl.loop(1, 2 * M)
    def _(k):
        terms_copy(k).start()

    terms_in[me] = terms[rows_at(t * share, share)]

    def sib_copy(c):
        return remote(sib_out.at[c], sib_in.at[c], sib_ss.at[c], sib_rs.at[c], sibling)

    def x_copy(c):
        return remote(x_out.at[c], x_in.at[c], x_ss.at[c], x_rs.at[c], across)

    def add_sibling(c):
        sib_copy(c).wait_recv()
        total = own[c] + sib_in[c].astype(jnp.float32)

        @pl.when(c < chunks)
        def _():
            x_out[jnp.minimum(c, chunks - 1)] = total.astype(jnp.bfloat16)
            x_copy(jnp.minimum(c, chunks - 1)).start()

        @pl.when(c >= chunks)
        def _():
            own[c] = total

    @pl.loop(0, 2 * chunks)
    def _(c):
        w_copy(c).wait()
        part = jnp.dot(acts_all[...], wbuf[c], preferred_element_type=jnp.float32)
        sib_out[c] = part[half:].astype(jnp.bfloat16)
        sib_copy(c).start()
        own[c] = part[:half].astype(jnp.bfloat16).astype(jnp.float32)

        @pl.when(c > 0)
        def _():
            add_sibling(c - 1)

        @pl.when(c == 2)
        def _():
            @pl.loop(1, 2 * M)
            def _(k):
                terms_arrival(k).wait_recv()

            low = jnp.sum(terms_in[...].astype(jnp.float32), axis=0).astype(jnp.bfloat16)
            shrink_own[...] = low
            shrink_half[rows_at(t * share, share)] = low

            @pl.loop(1, T)
            def _(k):
                shrink_copy(k).start()

    add_sibling(2 * chunks - 1)
    up_across.wait_recv()
    up_forward.start()

    @pl.loop(1, T)
    def _(k):
        shrink_arrival(k).wait_recv()

    slot_own = (ids_own + s) % 2 * 2 + (ids_own // 2 + dp) % 2
    low = shrink_half[...]
    lane_slot = lax.broadcasted_iota(jnp.int32, (half, 4 * rank), 1) // rank
    scat[...] = jnp.where(
        slot_own == lane_slot, jnp.concatenate([low] * 4, axis=1).astype(jnp.float32), 0.0
    ).astype(jnp.bfloat16)
    up_local.wait()
    rd_local.wait()
    up_beside.wait_recv()
    rd_arrival.wait_recv()
    up_forward.wait_recv()
    score_acc[...] = jnp.zeros_like(score_acc)

    def columns_of(j):
        return pl.ds(pl.multiple_of(j * chunk, 128), chunk)

    @pl.loop(0, chunks)
    def _(j):
        x_copy(j).wait_recv()
        base = own[chunks + j] + x_in[j].astype(jnp.float32)
        widened = jnp.dot(
            scat[...], upbuf[:, columns_of(j)], preferred_element_type=jnp.float32
        ).astype(jnp.bfloat16)
        policy = base + adapter_scale * widened.astype(jnp.float32)
        read = rd[:, columns_of(j)].astype(jnp.float32)
        sig = jax.nn.sigmoid(policy)
        gain = read * (policy * sig - base * jax.nn.sigmoid(base))
        total = score_acc[...]
        for i in range(chunk // 128):
            total = total + gain[:, i * 128 : (i + 1) * 128]
        score_acc[...] = total
        own[chunks + j] = read * (sig * (1.0 + policy * (1.0 - sig)))

    margin_own[...] = jnp.broadcast_to(
        jnp.sum(score_acc[...].T, axis=0, keepdims=True), margin_own.shape
    )

    def margin_copy(k):
        number, d, z = same_sub(k)
        return remote(
            margin_own, margin_in.at[mine], margin_ss.at[number], margin_rs.at[mine], to_device(d, z, s)
        )

    def margin_arrival(k):
        number, d, z = same_sub(k)
        return remote(
            margin_own, margin_in.at[number], margin_ss.at[number], margin_rs.at[number], sibling
        )

    @pl.loop(1, M)
    def _(k):
        margin_copy(k).start()

    margin_in[mine] = margin_own[...]

    @pl.loop(0, chunks)
    def _(j):
        x_copy(j).wait_send()

    @pl.loop(0, 2 * chunks)
    def _(c):
        sib_copy(c).wait_send()

    @pl.loop(0, T - 1)
    def _(i):
        @pl.when(when_up(i))
        def _():
            acts_up(i).wait_send()

        @pl.when(when_down(i))
        def _():
            acts_downward(i).wait_send()

    @pl.loop(1, T)
    def _(k):
        shrink_copy(k).wait_send()

    @pl.loop(1, 2 * M)
    def _(k):
        terms_copy(k).wait_send()

    up_across.wait_send()
    up_beside.wait_send()
    up_forward.wait_send()
    rd_across.wait_send()
    pick_across.wait_send()
    acts_back.wait()
    pick_arrival.wait_recv()

    @pl.loop(1, M)
    def _(k):
        margin_arrival(k).wait_recv()

    margin_rows = jnp.sum(margin_in[...], axis=0)[0:1]
    picks = pick[...].reshape(-1, half)
    margin = beta_pref * jnp.sum(picks * margin_rows, axis=1, keepdims=True)
    weight = beta_pref * jax.nn.sigmoid(-margin)
    row_grad = -jnp.sum(picks * weight, axis=0, keepdims=True)
    row_column = jnp.broadcast_to(row_grad, (half, half)).T[:, 0:1]
    rank_acc[...] = jnp.zeros_like(rank_acc)

    def ug_copy(j):
        return remote(ug_out.at[j], ug_in.at[j], ug_ss.at[j], ug_rs.at[j], sibling)

    def gx_copy(j):
        return remote(gx_out.at[j], gx_in.at[j], gx_ss.at[j], gx_rs.at[j], across)

    def out_copy(j):
        off = pl.multiple_of(dp * span + j * chunk, 128)
        return pltpu.make_async_copy(gown.at[j], upg.at[:, pl.ds(off, chunk)], out_sem.at[j])

    def out_copy_across(j):
        off = pl.multiple_of((1 - dp) * span + j * chunk, 128)
        return pltpu.make_async_copy(
            gx_in.at[j], upg.at[:, pl.ds(off, chunk)], out_sem.at[chunks + j]
        )

    def add_up(j):
        ug_copy(j).wait_recv()
        total = (ug_own[j] + ug_in[j].astype(jnp.float32)).astype(jnp.bfloat16)
        gx_out[j] = total[group:]
        gx_copy(j).start()
        gown[j] = total[:group]
        out_copy(j).start()

    @pl.loop(0, chunks)
    def _(j):
        grad = (row_column * own[chunks + j]).astype(jnp.bfloat16)
        grads[j] = grad
        rank_acc[...] += lax.dot_general(
            grad,
            upbuf[:, columns_of(j)],
            (((1,), (1,)), ((), ())),
            preferred_element_type=jnp.float32,
        )

    every = jnp.where(slot_own == lane_slot, rank_acc[...], 0.0)
    rank_part[...] = sum(every[:, i * rank : (i + 1) * rank] for i in range(4))

    def rank_copy(k):
        number, d, z = same_sub(k)
        return remote(
            rank_part.at[rows_at(z * share, share)],
            rank_in.at[mine],
            rank_ss.at[number],
            rank_rs.at[mine],
            to_device(d, z, s),
        )

    def rank_arrival(k):
        number, d, z = same_sub(k)
        return remote(
            rank_part.at[0:share], rank_in.at[number], rank_ss.at[number], rank_rs.at[number], sibling
        )

    @pl.loop(1, M)
    def _(k):
        rank_copy(k).start()

    rank_in[mine] = rank_part[rows_at(t * share, share)]

    @pl.loop(0, chunks)
    def _(j):
        ug = lax.dot_general(
            scat[...], grads[j], (((0,), (0,)), ((), ())), preferred_element_type=jnp.float32
        )
        ug = adapter_scale * ug
        ug_out[j] = ug[half:].astype(jnp.bfloat16)
        ug_copy(j).start()
        ug_own[j] = ug[:half]

        @pl.when(j > 0)
        def _():
            add_up(j - 1)

    add_up(chunks - 1)

    @pl.loop(1, M)
    def _(k):
        rank_arrival(k).wait_recv()

    low = (adapter_scale * jnp.sum(rank_in[...], axis=0)).astype(jnp.bfloat16)
    rank_own[...] = low

    def on_side(k):
        number = lax.rem(t * 2 + s + k, M)
        return number, number // 2, lax.rem(number, 2)

    def all_copy(k):
        number, z, c = on_side(k)
        block = jnp.where(c == s, 0, T) + t
        return remote(
            rank_own,
            rank_all.at[rows_at(block * share, share)],
            all_ss.at[number],
            all_rs.at[t * 2 + s],
            to_device(dp, z, c),
        )

    def all_arrival(k):
        number, z, c = on_side(k)
        block = jnp.where(c == s, 0, T) + z
        return remote(
            rank_own,
            rank_all.at[rows_at(block * share, share)],
            all_ss.at[number],
            all_rs.at[number],
            sibling,
        )

    @pl.loop(1, M)
    def _(k):
        all_copy(k).start()

    rank_all[rows_at(t * share, share)] = low

    @pl.loop(1, M)
    def _(k):
        margin_copy(k).wait_send()
        rank_copy(k).wait_send()

    @pl.loop(0, chunks)
    def _(j):
        ug_copy(j).wait_send()

    @pl.loop(1, M)
    def _(k):
        all_arrival(k).wait_recv()

    @pl.loop(1, M)
    def _(k):
        all_copy(k).wait_send()

    rank_out[...] = jnp.where(ids_all == t, rank_all[...].astype(jnp.float32), 0.0).astype(
        jnp.bfloat16
    )

    @pl.loop(0, chunks)
    def _(j):
        gx_copy(j).wait_recv()
        out_copy_across(j).start()

    @pl.loop(0, chunks)
    def _(j):
        gx_copy(j).wait_send()
        out_copy(j).wait()
        out_copy_across(j).wait()


def fast_body(
    acts,
    frozen_weight,
    adapter_down_maps,
    adapter_up_maps,
    down_first_moment,
    down_second_moment,
    up_first_moment,
    up_second_moment,
    readout,
    adapter_index_rows,
    preference_pair_rows,
):
    T = lax.axis_size("tensor")
    group, depth = acts.shape
    rows = T * group
    half = rows // 2
    columns = frozen_weight.shape[1]
    span = columns // 2
    rank = adapter_down_maps.shape[2]
    chunk = chunk_of(span)
    chunks = span // chunk
    M = 2 * T
    share = half // T
    bf16, f32 = jnp.bfloat16, jnp.float32
    V, dma = pltpu.VMEM, pltpu.SemaphoreType.DMA
    any_spec = pl.BlockSpec(memory_space=pl.ANY)
    vmem_spec = pl.BlockSpec(memory_space=pltpu.VMEM)
    up_grad, rank_masked, rows_all = pl.pallas_call(
        functools.partial(step_kernel, T, chunk),
        out_shape=(
            jax.ShapeDtypeStruct((rank, columns), bf16),
            jax.ShapeDtypeStruct((rows, rank), bf16),
            jax.ShapeDtypeStruct((rows, depth), bf16),
        ),
        in_specs=[any_spec] * 7,
        out_specs=(any_spec, vmem_spec, any_spec),
        scratch_shapes=[
            V((rows, depth), bf16),
            V((2 * chunks, depth, chunk), bf16),
            V((2 * chunks, half, chunk), f32),
            V((2 * chunks, half, chunk), bf16),
            V((2 * chunks, half, chunk), bf16),
            V((chunks, half, chunk), bf16),
            V((chunks, half, chunk), bf16),
            V((4 * rank, span), bf16),
            V((half, span), bf16),
            V((rows, rank), bf16),
            V((2 * M, share, rank), bf16),
            V((share, rank), bf16),
            V((half, rank), bf16),
            V((half, 4 * rank), bf16),
            V((2, group // 2, half), f32),
            V((8, half), f32),
            V((M, 8, half), f32),
            V((8, 128), f32),
            V((chunks, half, chunk), f32),
            V((chunks, half, chunk), bf16),
            V((chunks, half, chunk), bf16),
            V((chunks, group, chunk), bf16),
            V((chunks, group, chunk), bf16),
            V((chunks, group, chunk), bf16),
            V((half, rank), f32),
            V((M, share, rank), f32),
            V((share, rank), bf16),
            V((rows, rank), bf16),
            V((half, 4 * rank), f32),
            V((half, 128), f32),
            V((rank, depth), bf16),
            V((1, rows), jnp.int32),
            V((2, group // 2), jnp.int32),
            V((chunks, half, chunk), bf16),
            dma((2 * T,)), dma((T,)), dma((2 * chunks,)), dma((7,)),
            dma((2 * chunks,)), dma((2 * chunks,)), dma((chunks,)), dma((chunks,)),
            dma((5,)), dma((5,)), dma((2 * M,)), dma((2 * M,)),
            dma((T,)), dma((T,)), dma((M,)), dma((M,)),
            dma((chunks,)), dma((chunks,)), dma((chunks,)), dma((chunks,)),
            dma((2 * chunks,)), dma((M,)), dma((M,)), dma((M,)), dma((M,)),
        ],
        compiler_params=pltpu.CompilerParams(
            collective_id=0, has_side_effects=True, vmem_limit_bytes=40 * 1024 * 1024
        ),
    )(
        *(
            pltpu.with_memory_space_constraint(held, pltpu.HBM)
            for held in (
                acts,
                frozen_weight,
                adapter_down_maps[0].T,
                adapter_up_maps[0],
                readout,
                adapter_index_rows.T,
                preference_pair_rows.T,
            )
        )
    )
    down_gradient = jnp.einsum("rd,rk->dk", rows_all, rank_masked, preferred_element_type=f32)[None]
    up_gradient = up_grad.astype(f32)[None]
    return moment_update_step(
        adapter_down_maps, down_first_moment, down_second_moment, down_gradient
    ) + moment_update_step(adapter_up_maps, up_first_moment, up_second_moment, up_gradient)


def chunk_of(span):
    return next((c for c in (640, 512, 384, 256, 128) if span % c == 0), 0)


def fits(mesh, args):
    sizes = mesh.shape
    T = sizes["tensor"]
    if sizes["dp"] != 2 or sizes["sub"] != 2 or T != 4:
        return False
    rows = args[0].shape[0] // sizes["parts"]
    span = args[1].shape[1] // (2 * T)
    rank = args[2].shape[2]
    return rows == 256 and rank == 64 and args[2].shape[0] == 4 * sizes["parts"] and chunk_of(span) > 0


def solution(mesh):
    placed = (
        P(("parts", "tensor"), ("dp", "sub")),
        P(("dp", "sub"), "tensor"),
        P(("parts", "tensor"), ("dp", "sub"), None),
        P(("parts", "dp", "sub"), None, "tensor"),
        P(("parts", "tensor"), ("dp", "sub"), None),
        P(("parts", "tensor"), ("dp", "sub"), None),
        P(("parts", "dp", "sub"), None, "tensor"),
        P(("parts", "dp", "sub"), None, "tensor"),
        P(("parts", "dp", "sub"), "tensor"),
        P("parts", None),
        P(("parts", "dp", "sub"), None),
    )
    def run(*args):
        return sharded(fast_body if fits(mesh, args) else body)(*args)

    sharded = lambda inner: jax.shard_map(
        inner,
        mesh=mesh,
        in_specs=placed,
        out_specs=(
            P(("parts", "tensor"), ("dp", "sub"), None),
            P(("parts", "tensor"), ("dp", "sub"), None),
            P(("parts", "tensor"), ("dp", "sub"), None),
            P(("parts", "dp", "sub"), None, "tensor"),
            P(("parts", "dp", "sub"), None, "tensor"),
            P(("parts", "dp", "sub"), None, "tensor"),
        ),
        check_vma=False,
    )
    return run
```

```python
import functools

import jax
import jax.numpy as jnp
from jax import lax
from jax.experimental import pallas as pl
from jax.experimental.pallas import tpu as pltpu
from jax.sharding import PartitionSpec as P

adapter_scale = 2.0
beta_pref = 0.1
learn_rate = 0.001
first_decay = 0.9
second_decay = 0.95
first_fix = 1.0 - 2.656139888758747e-05
second_fix = 1.0 - 0.005920529220334
adam_eps = 1e-08


def swish_slope(pre_act):
    sigmoid_of = jax.nn.sigmoid(pre_act)
    return sigmoid_of * (1.0 + pre_act * (1.0 - sigmoid_of))


def moment_update_step(param, mean_old, square_old, grad):
    new_mean = first_decay * mean_old + (1.0 - first_decay) * grad
    new_square = second_decay * square_old + (1.0 - second_decay) * grad * grad
    update_step = new_mean / first_fix / (jnp.sqrt(new_square / second_fix) + adam_eps)
    new_param = (param.astype(jnp.float32) - learn_rate * update_step).astype(jnp.bfloat16)
    return (new_param, new_mean, new_square)


def body(
    acts,
    frozen_weight,
    adapter_down_maps,
    adapter_up_maps,
    down_first_moment,
    down_second_moment,
    up_first_moment,
    up_second_moment,
    readout,
    adapter_index_rows,
    preference_pair_rows,
):
    group_count = lax.axis_size(("dp", "sub"))
    group_index = lax.axis_index(("dp", "sub"))
    tensor_index = lax.axis_index("tensor")
    reduced_rank_output = adapter_down_maps.shape[2]
    local_down_maps = adapter_down_maps.shape[0]
    local_up_maps = adapter_up_maps.shape[0]
    adapters = local_up_maps * group_count
    group_rows = readout.shape[0]
    columns = readout.shape[1]
    ids_all = adapter_index_rows[:, 0]
    catalog = jnp.arange(adapters, dtype=jnp.int32)
    member_all = (ids_all[:, None] == catalog[None, :]).astype(jnp.float32)
    member_mine = lax.dynamic_slice_in_dim(
        member_all, tensor_index * local_down_maps, local_down_maps, 1
    )
    rows_all = lax.all_gather(acts, "tensor", axis=0, tiled=True)
    base_part = jnp.dot(rows_all, frozen_weight, preferred_element_type=jnp.float32)
    down_maps_total = lax.all_gather(adapter_down_maps, "tensor", axis=0, tiled=True)
    products = jnp.einsum(
        "rd,adk->rak", rows_all, down_maps_total, preferred_element_type=jnp.float32
    )
    shrink_part = jnp.sum(products * member_all[:, :, None], axis=1)
    base_terms = base_part.astype(jnp.bfloat16).reshape(group_count, group_rows, columns)
    shrink_terms = shrink_part.astype(jnp.bfloat16).reshape(
        group_count, group_rows, reduced_rank_output
    )
    base_arrived, shrink_arrived = (
        lax.all_to_all(base_terms, ("dp", "sub"), split_axis=0, concat_axis=0, tiled=True),
        lax.all_to_all(shrink_terms, ("dp", "sub"), split_axis=0, concat_axis=0, tiled=True),
    )
    frozen_sum = jnp.sum(base_arrived.astype(jnp.float32), axis=0)
    shrink = jnp.sum(shrink_arrived.astype(jnp.float32), axis=0)
    shrink_low = shrink.astype(jnp.bfloat16)
    my_ids = lax.dynamic_slice_in_dim(ids_all, group_index * group_rows, group_rows, 0)
    capacity = 2 * group_rows // adapters
    member_int = (my_ids[:, None] == catalog[None, :]).astype(jnp.int32)
    before = jnp.cumsum(member_int, axis=0) - member_int
    slot_index = jnp.sum(before * member_int, axis=1)
    position = my_ids * capacity + slot_index
    placing = (
        position[None, :] == jnp.arange(adapters * capacity, dtype=jnp.int32)[:, None]
    ).astype(jnp.bfloat16)
    outgoing = (
        jnp.dot(placing, shrink_low, preferred_element_type=jnp.float32)
        .astype(jnp.bfloat16)
        .reshape(adapters, capacity, reduced_rank_output)
    )
    received = lax.all_to_all(outgoing, ("dp", "sub"), split_axis=0, concat_axis=0, tiled=True)
    slot_count = received.shape[1]
    grid_rank = received.reshape(group_count, local_up_maps, slot_count, reduced_rank_output)
    expanded = jnp.einsum(
        "gjcr,jrf->gjcf", grid_rank, adapter_up_maps, preferred_element_type=jnp.float32
    ).astype(jnp.bfloat16)
    returned = lax.all_to_all(
        expanded.reshape(group_count * local_up_maps, slot_count, columns),
        ("dp", "sub"),
        split_axis=0,
        concat_axis=0,
        tiled=True,
    )
    returned, arrived = (returned, received)
    widen_rows = jnp.dot(
        placing.T,
        returned.reshape(adapters * capacity, columns),
        preferred_element_type=jnp.float32,
    ).astype(jnp.bfloat16)
    policy_scores = frozen_sum + adapter_scale * widen_rows.astype(jnp.float32)
    read_float = readout.astype(jnp.float32)
    score_policy, score_base = lax.psum(
        (
            jnp.sum(read_float * jax.nn.silu(policy_scores), axis=1),
            jnp.sum(read_float * jax.nn.silu(frozen_sum), axis=1),
        ),
        "tensor",
    )
    margin_rows = score_policy - score_base
    row_number = jnp.arange(group_rows, dtype=jnp.int32)
    pick_chosen = (preference_pair_rows[:, 0:1] == row_number[None, :]).astype(jnp.float32)
    pick_rejected = (preference_pair_rows[:, 1:2] == row_number[None, :]).astype(jnp.float32)
    margin = beta_pref * (
        jnp.sum(pick_chosen * margin_rows[None, :], axis=1)
        - jnp.sum(pick_rejected * margin_rows[None, :], axis=1)
    )
    weight = beta_pref * jax.nn.sigmoid(-margin)
    row_grad = jnp.sum((pick_rejected - pick_chosen) * weight[:, None], axis=0)
    output_gradient = (row_grad[:, None] * read_float * swish_slope(policy_scores)).astype(
        jnp.bfloat16
    )
    outgoing_grad = (
        jnp.dot(placing, output_gradient, preferred_element_type=jnp.float32)
        .astype(jnp.bfloat16)
        .reshape(adapters, capacity, columns)
    )
    arrived_grad = lax.all_to_all(
        outgoing_grad, ("dp", "sub"), split_axis=0, concat_axis=0, tiled=True
    )
    grid_rank = arrived.reshape(group_count, local_up_maps, capacity, reduced_rank_output)
    grid_grad = arrived_grad.reshape(group_count, local_up_maps, capacity, columns)
    up_gradient = adapter_scale * jnp.einsum(
        "gjcr,gjcf->jrf", grid_rank, grid_grad, preferred_element_type=jnp.float32
    )
    rank_slots = jnp.einsum(
        "gjcf,jrf->gjcr", grid_grad, adapter_up_maps, preferred_element_type=jnp.float32
    )
    rank_back = lax.all_to_all(
        rank_slots.reshape(group_count * local_up_maps, capacity, reduced_rank_output).astype(
            jnp.bfloat16
        ),
        ("dp", "sub"),
        split_axis=0,
        concat_axis=0,
        tiled=True,
    ).astype(jnp.float32)
    rank_portion = jnp.dot(
        placing.astype(jnp.float32).T,
        rank_back.reshape(adapters * capacity, reduced_rank_output),
        precision=lax.Precision.HIGHEST,
    )
    rank_gradient = (adapter_scale * lax.psum(rank_portion, "tensor")).astype(jnp.bfloat16)
    rank_all = lax.all_gather(rank_gradient, ("dp", "sub"), axis=0, tiled=True)
    spread_back = (member_mine[:, :, None] * rank_all.astype(jnp.float32)[:, None, :]).astype(
        jnp.bfloat16
    )
    down_gradient = jnp.einsum(
        "rd,rjk->jdk", rows_all, spread_back, preferred_element_type=jnp.float32
    )
    updated_down_maps, updated_down_first, updated_down_second = moment_update_step(
        adapter_down_maps, down_first_moment, down_second_moment, down_gradient
    )
    updated_up_maps, updated_up_first, updated_up_second = moment_update_step(
        adapter_up_maps, up_first_moment, up_second_moment, up_gradient
    )
    return (
        updated_down_maps,
        updated_down_first,
        updated_down_second,
        updated_up_maps,
        updated_up_first,
        updated_up_second,
    )


def to_device(dp, t, s):
    return {"dp": dp, "tensor": t, "sub": s}


def remote(src, dst, send_sem, recv_sem, device):
    return pltpu.make_async_remote_copy(
        src_ref=src,
        dst_ref=dst,
        send_sem=send_sem,
        recv_sem=recv_sem,
        device_id=device,
        device_id_type=pl.DeviceIdType.MESH,
    )


def rows_at(start, size):
    return pl.ds(pl.multiple_of(start, size), size)


def step_kernel(
    T, chunk, acts, w, down_in, up, readout, ids_in, pairs_in,
    upg, rank_out, acts_out,
    acts_all, wbuf, own, sib_out, sib_in, x_out, x_in, upbuf, rd,
    terms, terms_in, shrink_own, shrink_half, scat, pick,
    margin_own, margin_in, grad_out, ug_own, ug_out, ug_in, gx_out, gx_in, gown,
    rank_part, rank_in, rank_own, rank_all, rank_acc, score_acc, down, ids, pairs, grads,
    acts_ss, acts_rs, w_sem, local_sem, sib_ss, sib_rs, x_ss, x_rs,
    mat_ss, mat_rs, terms_ss, terms_rs, shrink_ss, shrink_rs, margin_ss, margin_rs,
    ug_ss, ug_rs, gx_ss, gx_rs, out_sem, rank_ss, rank_rs, all_ss, all_rs,
):
    dp, t, s = lax.axis_index("dp"), lax.axis_index("tensor"), lax.axis_index("sub")
    rows = acts_all.shape[0]
    half = rows // 2
    group = half // 2
    columns = w.shape[1]
    span = columns // 2
    chunks = span // chunk
    rank = down.shape[0]
    share = half // T
    M = 2 * T
    mine = dp * T + t
    me = mine * 2 + s
    sibling = to_device(dp, t, 1 - s)
    across = to_device(1 - dp, t, s)
    here = pl.multiple_of(dp * span, 128)
    there = pl.multiple_of((1 - dp) * span, 128)

    def w_copy(c):
        base = jnp.where(c < chunks, 1 - dp, dp) * span
        off = base + lax.rem(c, chunks) * chunk
        return pltpu.make_async_copy(
            w.at[:, pl.ds(pl.multiple_of(off, 128), chunk)], wbuf.at[c], w_sem.at[c]
        )

    def device_at(k):
        number = lax.rem(me + k, 2 * M)
        return number, number // (2 * T), lax.rem(number // 2, T), lax.rem(number, 2)

    ids_local = pltpu.make_async_copy(ids_in, ids, local_sem.at[4])
    pairs_local = pltpu.make_async_copy(pairs_in, pairs, local_sem.at[5])
    down_local = pltpu.make_async_copy(down_in, down, local_sem.at[6])
    ids_local.start()
    pairs_local.start()
    down_local.start()

    @pl.loop(0, 2)
    def _(c):
        w_copy(c).start()

    up_local = pltpu.make_async_copy(up.at[:, pl.ds(here, span)], upbuf.at[0:group], local_sem.at[0])
    rd_local = pltpu.make_async_copy(
        readout.at[:, pl.ds(here, span)], rd.at[rows_at(dp * group, group)], local_sem.at[1]
    )
    own_slot = rows_at((lax.rem(t + s, 2) * 2 + t // 2) * group, group)
    acts_local = pltpu.make_async_copy(acts, acts_all.at[own_slot], local_sem.at[2])
    up_local.start()
    rd_local.start()
    acts_local.start()

    barrier = pltpu.get_barrier_semaphore()

    @pl.loop(1, 2 * M)
    def _(k):
        _, d, z, c = device_at(k)
        pl.semaphore_signal(
            barrier, inc=1, device_id=to_device(d, z, c), device_id_type=pl.DeviceIdType.MESH
        )

    pl.semaphore_wait(barrier, 2 * M - 1)

    def acts_slot(z):
        return acts_all.at[rows_at((lax.rem(z + s, 2) * 2 + z // 2) * group, group)]

    def acts_up(i):
        block = t - i
        return remote(
            acts_slot(block), acts_slot(block), acts_ss.at[i], acts_rs.at[block], to_device(dp, t + 1, s)
        )

    def acts_downward(i):
        block = t + i
        return remote(
            acts_slot(block),
            acts_slot(block),
            acts_ss.at[T + i],
            acts_rs.at[block],
            to_device(dp, t - 1, s),
        )

    def acts_arrival(block):
        return remote(acts_slot(block), acts_slot(block), acts_ss.at[0], acts_rs.at[block], sibling)

    def when_up(i):
        return (t - i >= 0) & (t + 1 < T)

    def when_down(i):
        return (t + i < T) & (t >= 1)

    acts_local.wait()

    @pl.when(when_up(0))
    def _():
        acts_up(0).start()

    @pl.when(when_down(0))
    def _():
        acts_downward(0).start()

    up_across = remote(
        up.at[:, pl.ds(there, span)], upbuf.at[group : 2 * group], mat_ss.at[0], mat_rs.at[0], across
    )
    up_beside = remote(
        up.at[:, pl.ds(here, span)], upbuf.at[2 * group : 3 * group], mat_ss.at[1], mat_rs.at[1], sibling
    )
    up_forward = remote(
        upbuf.at[group : 2 * group], upbuf.at[3 * group : 4 * group], mat_ss.at[2], mat_rs.at[2], sibling
    )
    rd_across = remote(
        readout.at[:, pl.ds(there, span)],
        rd.at[rows_at(dp * group, group)],
        mat_ss.at[3],
        mat_rs.at[3],
        across,
    )
    pick_across = remote(pick.at[dp], pick.at[dp], mat_ss.at[4], mat_rs.at[4], across)
    pick_arrival = remote(pick.at[1 - dp], pick.at[1 - dp], mat_ss.at[4], mat_rs.at[4], across)
    rd_arrival = remote(
        readout.at[:, pl.ds(there, span)],
        rd.at[rows_at((1 - dp) * group, group)],
        mat_ss.at[3],
        mat_rs.at[3],
        across,
    )
    up_across.start()
    rd_across.start()
    up_beside.start()

    @pl.loop(2, 2 * chunks)
    def _(c):
        w_copy(c).start()

    pairs_local.wait()
    row_line = lax.broadcasted_iota(jnp.int32, (half, group // 2), 0) - dp * group
    pick[dp] = (
        (pairs[0:1] == row_line).astype(jnp.float32) - (pairs[1:2] == row_line).astype(jnp.float32)
    ).T
    pick_across.start()
    ids_local.wait()
    ids_column = jnp.broadcast_to(ids[...].astype(jnp.float32), (128, rows)).T[:, 0:1]
    ids_column = ids_column.astype(jnp.int32)
    first = [ids_column[g * group : (g + 1) * group] for g in range(4)]
    ids_even = jnp.concatenate([first[0], first[2]], axis=0)
    ids_odd = jnp.concatenate([first[1], first[3]], axis=0)
    on_odd = jnp.full((half, 1), s, jnp.int32) == 1
    ids_own = jnp.where(on_odd, ids_odd, ids_even)
    ids_sib = jnp.where(on_odd, ids_even, ids_odd)
    ids_all = jnp.concatenate([ids_own, ids_sib], axis=0)

    down_local.wait()

    @pl.loop(1, T)
    def _(i):
        @pl.when(t - i >= 0)
        def _():
            acts_arrival(t - i).wait_recv()

            @pl.when(when_up(i))
            def _():
                acts_up(i).start()

        @pl.when(t + i < T)
        def _():
            acts_arrival(t + i).wait_recv()

            @pl.when(when_down(i))
            def _():
                acts_downward(i).start()

    acts_back = pltpu.make_async_copy(acts_all, acts_out, local_sem.at[3])
    acts_back.start()
    products = lax.dot_general(
        acts_all[...], down[...], (((1,), (1,)), ((), ())), preferred_element_type=jnp.float32
    )
    terms[...] = jnp.where(ids_all == t, products, 0.0).astype(jnp.bfloat16)

    def terms_copy(k):
        number, d, z, c = device_at(k)
        block = jnp.where(c == s, 0, T) + z
        return remote(
            terms.at[rows_at(block * share, share)],
            terms_in.at[me],
            terms_ss.at[number],
            terms_rs.at[me],
            to_device(d, z, c),
        )

    def terms_arrival(k):
        number, d, z, c = device_at(k)
        return remote(
            terms.at[0:share], terms_in.at[number], terms_ss.at[number], terms_rs.at[number], sibling
        )

    def same_sub(k):
        number = lax.rem(mine + k, M)
        return number, number // T, lax.rem(number, T)

    def shrink_copy(k):
        z = lax.rem(t + k, T)
        return remote(
            shrink_own,
            shrink_half.at[rows_at(t * share, share)],
            shrink_ss.at[z],
            shrink_rs.at[t],
            to_device(dp, z, s),
        )

    def shrink_arrival(k):
        z = lax.rem(t + k, T)
        return remote(
            shrink_own,
            shrink_half.at[rows_at(z * share, share)],
            shrink_ss.at[z],
            shrink_rs.at[z],
            sibling,
        )

    @pl.loop(1, 2 * M)
    def _(k):
        terms_copy(k).start()

    terms_in[me] = terms[rows_at(t * share, share)]

    def sib_copy(c):
        return remote(sib_out.at[c], sib_in.at[c], sib_ss.at[c], sib_rs.at[c], sibling)

    def x_copy(c):
        return remote(x_out.at[c], x_in.at[c], x_ss.at[c], x_rs.at[c], across)

    def add_sibling(c):
        sib_copy(c).wait_recv()
        total = own[c] + sib_in[c].astype(jnp.float32)

        @pl.when(c < chunks)
        def _():
            x_out[jnp.minimum(c, chunks - 1)] = total.astype(jnp.bfloat16)
            x_copy(jnp.minimum(c, chunks - 1)).start()

        @pl.when(c >= chunks)
        def _():
            own[c] = total

    @pl.loop(0, 2 * chunks)
    def _(c):
        w_copy(c).wait()
        part = jnp.dot(acts_all[...], wbuf[c], preferred_element_type=jnp.float32)
        sib_out[c] = part[half:].astype(jnp.bfloat16)
        sib_copy(c).start()
        own[c] = part[:half].astype(jnp.bfloat16).astype(jnp.float32)

        @pl.when(c > 0)
        def _():
            add_sibling(c - 1)

        @pl.when(c == 2)
        def _():
            @pl.loop(1, 2 * M)
            def _(k):
                terms_arrival(k).wait_recv()

            low = jnp.sum(terms_in[...].astype(jnp.float32), axis=0).astype(jnp.bfloat16)
            shrink_own[...] = low
            shrink_half[rows_at(t * share, share)] = low

            @pl.loop(1, T)
            def _(k):
                shrink_copy(k).start()

    add_sibling(2 * chunks - 1)
    up_across.wait_recv()
    up_forward.start()

    @pl.loop(1, T)
    def _(k):
        shrink_arrival(k).wait_recv()

    slot_own = (ids_own + s) % 2 * 2 + (ids_own // 2 + dp) % 2
    low = shrink_half[...]
    lane_slot = lax.broadcasted_iota(jnp.int32, (half, 4 * rank), 1) // rank
    scat[...] = jnp.where(
        slot_own == lane_slot, jnp.concatenate([low] * 4, axis=1).astype(jnp.float32), 0.0
    ).astype(jnp.bfloat16)
    up_local.wait()
    rd_local.wait()
    up_beside.wait_recv()
    rd_arrival.wait_recv()
    up_forward.wait_recv()
    score_acc[...] = jnp.zeros_like(score_acc)

    def columns_of(j):
        return pl.ds(pl.multiple_of(j * chunk, 128), chunk)

    @pl.loop(0, chunks)
    def _(j):
        x_copy(j).wait_recv()
        base = own[chunks + j] + x_in[j].astype(jnp.float32)
        widened = jnp.dot(
            scat[...], upbuf[:, columns_of(j)], preferred_element_type=jnp.float32
        ).astype(jnp.bfloat16)
        policy = base + adapter_scale * widened.astype(jnp.float32)
        read = rd[:, columns_of(j)].astype(jnp.float32)
        sig = jax.nn.sigmoid(policy)
        gain = read * (policy * sig - base * jax.nn.sigmoid(base))
        total = score_acc[...]
        for i in range(chunk // 128):
            total = total + gain[:, i * 128 : (i + 1) * 128]
        score_acc[...] = total
        own[chunks + j] = read * (sig * (1.0 + policy * (1.0 - sig)))

    margin_own[...] = jnp.broadcast_to(
        jnp.sum(score_acc[...].T, axis=0, keepdims=True), margin_own.shape
    )

    def margin_copy(k):
        number, d, z = same_sub(k)
        return remote(
            margin_own, margin_in.at[mine], margin_ss.at[number], margin_rs.at[mine], to_device(d, z, s)
        )

    def margin_arrival(k):
        number, d, z = same_sub(k)
        return remote(
            margin_own, margin_in.at[number], margin_ss.at[number], margin_rs.at[number], sibling
        )

    @pl.loop(1, M)
    def _(k):
        margin_copy(k).start()

    margin_in[mine] = margin_own[...]

    @pl.loop(0, chunks)
    def _(j):
        x_copy(j).wait_send()

    @pl.loop(0, 2 * chunks)
    def _(c):
        sib_copy(c).wait_send()

    @pl.loop(0, T - 1)
    def _(i):
        @pl.when(when_up(i))
        def _():
            acts_up(i).wait_send()

        @pl.when(when_down(i))
        def _():
            acts_downward(i).wait_send()

    @pl.loop(1, T)
    def _(k):
        shrink_copy(k).wait_send()

    @pl.loop(1, 2 * M)
    def _(k):
        terms_copy(k).wait_send()

    up_across.wait_send()
    up_beside.wait_send()
    up_forward.wait_send()
    rd_across.wait_send()
    pick_across.wait_send()
    acts_back.wait()
    pick_arrival.wait_recv()

    @pl.loop(1, M)
    def _(k):
        margin_arrival(k).wait_recv()

    margin_rows = jnp.sum(margin_in[...], axis=0)[0:1]
    picks = pick[...].reshape(-1, half)
    margin = beta_pref * jnp.sum(picks * margin_rows, axis=1, keepdims=True)
    weight = beta_pref * jax.nn.sigmoid(-margin)
    row_grad = -jnp.sum(picks * weight, axis=0, keepdims=True)
    row_column = jnp.broadcast_to(row_grad, (half, half)).T[:, 0:1]
    rank_acc[...] = jnp.zeros_like(rank_acc)

    def ug_copy(j):
        return remote(ug_out.at[j], ug_in.at[j], ug_ss.at[j], ug_rs.at[j], sibling)

    def gx_copy(j):
        return remote(gx_out.at[j], gx_in.at[j], gx_ss.at[j], gx_rs.at[j], across)

    def out_copy(j):
        off = pl.multiple_of(dp * span + j * chunk, 128)
        return pltpu.make_async_copy(gown.at[j], upg.at[:, pl.ds(off, chunk)], out_sem.at[j])

    def out_copy_across(j):
        off = pl.multiple_of((1 - dp) * span + j * chunk, 128)
        return pltpu.make_async_copy(
            gx_in.at[j], upg.at[:, pl.ds(off, chunk)], out_sem.at[chunks + j]
        )

    def add_up(j):
        ug_copy(j).wait_recv()
        total = (ug_own[j] + ug_in[j].astype(jnp.float32)).astype(jnp.bfloat16)
        gx_out[j] = total[group:]
        gx_copy(j).start()
        gown[j] = total[:group]
        out_copy(j).start()

    def up_part(j):
        ug = lax.dot_general(
            scat[...], grads[j], (((0,), (0,)), ((), ())), preferred_element_type=jnp.float32
        )
        ug = adapter_scale * ug
        ug_out[j] = ug[half:].astype(jnp.bfloat16)
        ug_copy(j).start()
        ug_own[j] = ug[:half]

    grads[0] = (row_column * own[chunks]).astype(jnp.bfloat16)
    up_part(0)

    @pl.loop(0, chunks)
    def _(j):
        grad = (row_column * own[chunks + j]).astype(jnp.bfloat16)
        grads[j] = grad
        rank_acc[...] += lax.dot_general(
            grad,
            upbuf[:, columns_of(j)],
            (((1,), (1,)), ((), ())),
            preferred_element_type=jnp.float32,
        )

    every = jnp.where(slot_own == lane_slot, rank_acc[...], 0.0)
    rank_part[...] = sum(every[:, i * rank : (i + 1) * rank] for i in range(4))

    def rank_copy(k):
        number, d, z = same_sub(k)
        return remote(
            rank_part.at[rows_at(z * share, share)],
            rank_in.at[mine],
            rank_ss.at[number],
            rank_rs.at[mine],
            to_device(d, z, s),
        )

    def rank_arrival(k):
        number, d, z = same_sub(k)
        return remote(
            rank_part.at[0:share], rank_in.at[number], rank_ss.at[number], rank_rs.at[number], sibling
        )

    @pl.loop(1, M)
    def _(k):
        rank_copy(k).start()

    rank_in[mine] = rank_part[rows_at(t * share, share)]

    add_up(0)

    @pl.loop(1, chunks)
    def _(j):
        up_part(j)

        @pl.when(j > 1)
        def _():
            add_up(j - 1)

    add_up(chunks - 1)

    @pl.loop(1, M)
    def _(k):
        rank_arrival(k).wait_recv()

    low = (adapter_scale * jnp.sum(rank_in[...], axis=0)).astype(jnp.bfloat16)
    rank_own[...] = low

    def on_side(k):
        number = lax.rem(t * 2 + s + k, M)
        return number, number // 2, lax.rem(number, 2)

    def all_copy(k):
        number, z, c = on_side(k)
        block = jnp.where(c == s, 0, T) + t
        return remote(
            rank_own,
            rank_all.at[rows_at(block * share, share)],
            all_ss.at[number],
            all_rs.at[t * 2 + s],
            to_device(dp, z, c),
        )

    def all_arrival(k):
        number, z, c = on_side(k)
        block = jnp.where(c == s, 0, T) + z
        return remote(
            rank_own,
            rank_all.at[rows_at(block * share, share)],
            all_ss.at[number],
            all_rs.at[number],
            sibling,
        )

    @pl.loop(1, M)
    def _(k):
        all_copy(k).start()

    rank_all[rows_at(t * share, share)] = low

    @pl.loop(1, M)
    def _(k):
        margin_copy(k).wait_send()
        rank_copy(k).wait_send()

    @pl.loop(0, chunks)
    def _(j):
        ug_copy(j).wait_send()

    @pl.loop(1, M)
    def _(k):
        all_arrival(k).wait_recv()

    @pl.loop(1, M)
    def _(k):
        all_copy(k).wait_send()

    rank_out[...] = jnp.where(ids_all == t, rank_all[...].astype(jnp.float32), 0.0).astype(
        jnp.bfloat16
    )

    @pl.loop(0, chunks)
    def _(j):
        gx_copy(j).wait_recv()
        out_copy_across(j).start()

    @pl.loop(0, chunks)
    def _(j):
        gx_copy(j).wait_send()
        out_copy(j).wait()
        out_copy_across(j).wait()


def fast_body(
    acts,
    frozen_weight,
    adapter_down_maps,
    adapter_up_maps,
    down_first_moment,
    down_second_moment,
    up_first_moment,
    up_second_moment,
    readout,
    adapter_index_rows,
    preference_pair_rows,
):
    T = lax.axis_size("tensor")
    group, depth = acts.shape
    rows = T * group
    half = rows // 2
    columns = frozen_weight.shape[1]
    span = columns // 2
    rank = adapter_down_maps.shape[2]
    chunk = chunk_of(span)
    chunks = span // chunk
    M = 2 * T
    share = half // T
    bf16, f32 = jnp.bfloat16, jnp.float32
    V, dma = pltpu.VMEM, pltpu.SemaphoreType.DMA
    any_spec = pl.BlockSpec(memory_space=pl.ANY)
    vmem_spec = pl.BlockSpec(memory_space=pltpu.VMEM)
    up_grad, rank_masked, rows_all = pl.pallas_call(
        functools.partial(step_kernel, T, chunk),
        out_shape=(
            jax.ShapeDtypeStruct((rank, columns), bf16),
            jax.ShapeDtypeStruct((rows, rank), bf16),
            jax.ShapeDtypeStruct((rows, depth), bf16),
        ),
        in_specs=[any_spec] * 7,
        out_specs=(any_spec, vmem_spec, any_spec),
        scratch_shapes=[
            V((rows, depth), bf16),
            V((2 * chunks, depth, chunk), bf16),
            V((2 * chunks, half, chunk), f32),
            V((2 * chunks, half, chunk), bf16),
            V((2 * chunks, half, chunk), bf16),
            V((chunks, half, chunk), bf16),
            V((chunks, half, chunk), bf16),
            V((4 * rank, span), bf16),
            V((half, span), bf16),
            V((rows, rank), bf16),
            V((2 * M, share, rank), bf16),
            V((share, rank), bf16),
            V((half, rank), bf16),
            V((half, 4 * rank), bf16),
            V((2, group // 2, half), f32),
            V((8, half), f32),
            V((M, 8, half), f32),
            V((8, 128), f32),
            V((chunks, half, chunk), f32),
            V((chunks, half, chunk), bf16),
            V((chunks, half, chunk), bf16),
            V((chunks, group, chunk), bf16),
            V((chunks, group, chunk), bf16),
            V((chunks, group, chunk), bf16),
            V((half, rank), f32),
            V((M, share, rank), f32),
            V((share, rank), bf16),
            V((rows, rank), bf16),
            V((half, 4 * rank), f32),
            V((half, 128), f32),
            V((rank, depth), bf16),
            V((1, rows), jnp.int32),
            V((2, group // 2), jnp.int32),
            V((chunks, half, chunk), bf16),
            dma((2 * T,)), dma((T,)), dma((2 * chunks,)), dma((7,)),
            dma((2 * chunks,)), dma((2 * chunks,)), dma((chunks,)), dma((chunks,)),
            dma((5,)), dma((5,)), dma((2 * M,)), dma((2 * M,)),
            dma((T,)), dma((T,)), dma((M,)), dma((M,)),
            dma((chunks,)), dma((chunks,)), dma((chunks,)), dma((chunks,)),
            dma((2 * chunks,)), dma((M,)), dma((M,)), dma((M,)), dma((M,)),
        ],
        compiler_params=pltpu.CompilerParams(
            collective_id=0, has_side_effects=True, vmem_limit_bytes=40 * 1024 * 1024
        ),
    )(
        *(
            pltpu.with_memory_space_constraint(held, pltpu.HBM)
            for held in (
                acts,
                frozen_weight,
                adapter_down_maps[0].T,
                adapter_up_maps[0],
                readout,
                adapter_index_rows.T,
                preference_pair_rows.T,
            )
        )
    )
    down_gradient = jnp.einsum("rd,rk->dk", rows_all, rank_masked, preferred_element_type=f32)[None]
    up_gradient = up_grad.astype(f32)[None]
    return moment_update_step(
        adapter_down_maps, down_first_moment, down_second_moment, down_gradient
    ) + moment_update_step(adapter_up_maps, up_first_moment, up_second_moment, up_gradient)


def chunk_of(span):
    return next((c for c in (640, 512, 384, 256, 128) if span % c == 0), 0)


def fits(mesh, args):
    sizes = mesh.shape
    T = sizes["tensor"]
    if sizes["dp"] != 2 or sizes["sub"] != 2 or T != 4:
        return False
    rows = args[0].shape[0] // sizes["parts"]
    span = args[1].shape[1] // (2 * T)
    rank = args[2].shape[2]
    return rows == 256 and rank == 64 and args[2].shape[0] == 4 * sizes["parts"] and chunk_of(span) > 0


def solution(mesh):
    placed = (
        P(("parts", "tensor"), ("dp", "sub")),
        P(("dp", "sub"), "tensor"),
        P(("parts", "tensor"), ("dp", "sub"), None),
        P(("parts", "dp", "sub"), None, "tensor"),
        P(("parts", "tensor"), ("dp", "sub"), None),
        P(("parts", "tensor"), ("dp", "sub"), None),
        P(("parts", "dp", "sub"), None, "tensor"),
        P(("parts", "dp", "sub"), None, "tensor"),
        P(("parts", "dp", "sub"), "tensor"),
        P("parts", None),
        P(("parts", "dp", "sub"), None),
    )
    def run(*args):
        return sharded(fast_body if fits(mesh, args) else body)(*args)

    sharded = lambda inner: jax.shard_map(
        inner,
        mesh=mesh,
        in_specs=placed,
        out_specs=(
            P(("parts", "tensor"), ("dp", "sub"), None),
            P(("parts", "tensor"), ("dp", "sub"), None),
            P(("parts", "tensor"), ("dp", "sub"), None),
            P(("parts", "dp", "sub"), None, "tensor"),
            P(("parts", "dp", "sub"), None, "tensor"),
            P(("parts", "dp", "sub"), None, "tensor"),
        ),
        check_vma=False,
    )
    return run
```
